256 devices in a mesh: loop: 128 (over z, y, x_lo, core), rhs: 2 (over x_hi).
Axes of the slice: x: 4 (x_hi: 2, x_lo: 2; x = x_hi * 2 + x_lo), y: 4, z: 8, core: 2. Of those that a mesh axis runs over, the one named last changes fastest.
Arguments:
- signals: bfloat16 [128, 262144], P('rhs', 'loop'), may hold values from -6 to 6
- near_tiles: bfloat16 [1024, 8, 256, 256], P('loop', 'rhs'), may hold values from -0.125 to 0.125
- near_list: int32 [1024, 8], P('loop'), may hold values from 0 to 1023, as said below
- leaf_basis: bfloat16 [1024, 64, 256], P('loop'), may hold values from -0.375 to 0.375
- transfer: bfloat16 [1024, 64, 64], P('loop'), may hold values from -0.75 to 0.75
- parent: int32 [1024], P('loop'), may hold values from 0 to 255, as said below
- coupling: bfloat16 [1024, 64, 1536], P('loop'), may hold values from -0.15625 to 0.15625
- far_list: int32 [1024, 24], P('loop'), may hold values from 0 to 1023, as said below
- parent_coupling: bfloat16 [256, 64, 1024], P('loop'), may hold values from -0.1875 to 0.1875
- parent_far: int32 [256, 16], P('loop'), may hold values from 0 to 255, as said below
Outputs:
- potentials: bfloat16 [128, 262144], P('rhs', 'loop')
The draws below stay inside these ranges and needn't reach their ends.
Inputs may be any that keep to these rules, and one draw needn't show every extreme that they name: `near_list`: entry 0 of each row is the leaf itself; the other entries of a row are distinct leaves at most 4 leaves away from it along the closed cycle of 1024 leaves, on either side; in every device's rows some leaf names the leaves exactly 4 away on both sides. Leaves of one device have parents of that device only (ids d * 2 and d * 2 + 1), and the parent ids never decrease along a device's leaves; every parent has 1 to 7 consecutive leaves, and some parent of every device has exactly 7. `far_list`: leaf d * 8 + i lies on device d. Among all entries of the rows of one device's 8 leaves, at most 2 name leaves of any one device, and in every draw each device's rows name some device's leaves exactly 2 times. `parent_far`: parent d * 2 + i lies on device d. Among all entries of the rows of one device's 2 parents, at most 2 name parents of any one device, and in every draw each device's rows name some device's parents exactly 2 times.
All inputs are finite; a program needn't handle non-finite values.
Results may differ from the reference program's by a relative error of at most 0.011.
Values may be sent and summed in bfloat16 or wider, within the bound.
No kernel may reach another device: no remote copies, remote signals or barrier semaphores. Data moves between devices by JAX's collectives and lax.ppermute only.
A program may use at most 128 MiB of HBM per device.

```python
import jax
import jax.numpy as jnp
from jax import lax

B = 256
K = 64
R = 128
LEAF_DEV = 8
NEAR = 8
FAR = 24
PFAR = 16
REACH = 4
PAR_DEV = 2
LEAVES = 1024
PARENTS = 256
POINTS = 262144
CAP = 2
PCAP = 2
N_LOOP = 128


def capped_sources(key, groups, entries, peers, capacity, per_peer):
    key_popular, key_jitter, key_favourite, key_ties, key_shuffle, key_local = jax.random.split(key, 6)
    popular = jax.random.randint(key_popular, (peers,), 0, 4)
    jitter = jax.random.randint(key_jitter, (groups, peers), 0, 2)
    favourite = jax.random.randint(key_favourite, (groups,), 0, peers)
    peer_numbers = jnp.arange(peers)
    levels = jnp.where(peer_numbers[None, :] == favourite[:, None], 8, popular[None, :] + jitter)
    slot_total = peers * capacity
    slot_peer = jnp.arange(slot_total) // capacity
    tiebreak = jax.random.randint(key_ties, (groups, slot_total), 0, slot_total) * slot_total + jnp.arange(slot_total)[None, :]
    scores = levels[:, slot_peer] * (slot_total * slot_total) + tiebreak
    chosen = lax.top_k(scores, entries)[1]
    shuffle_keys = jax.random.randint(key_shuffle, (groups, entries), 0, entries) * entries + jnp.arange(entries)[None, :]
    shuffle = jnp.argsort(shuffle_keys, axis=1)
    chosen = jnp.take_along_axis(chosen, shuffle, axis=1)
    local_member = jax.random.randint(key_local, (groups, entries), 0, per_peer)
    return (chosen // capacity * per_peer + local_member).astype(jnp.int32)


def draw_far_list(key, part):
    key = jax.random.fold_in(key, 11)
    sources = capped_sources(key, N_LOOP, LEAF_DEV * FAR, N_LOOP, CAP, LEAF_DEV)
    return sources.reshape(LEAVES, FAR)


def draw_parent_far(key, part):
    key = jax.random.fold_in(key, 13)
    sources = capped_sources(key, N_LOOP, PAR_DEV * PFAR, N_LOOP, PCAP, PAR_DEV)
    return sources.reshape(PARENTS, PFAR)


def draw_parent(key, part):
    key = jax.random.fold_in(key, 17)
    key_split, key_forced, key_side = jax.random.split(key, 3)
    pair_count = LEAF_DEV // 8
    splits = jax.random.randint(key_split, (N_LOOP, pair_count), 1, 8)
    forced = jax.random.randint(key_forced, (N_LOOP,), 0, pair_count)
    forced_split = 1 + 6 * jax.random.randint(key_side, (N_LOOP,), 0, 2)
    splits = jnp.where(jnp.arange(pair_count)[None, :] == forced[:, None], forced_split[:, None], splits)
    positions = jnp.arange(8)
    second = (positions[None, None, :] >= splits[:, :, None]).astype(jnp.int32)
    device_base = (jnp.arange(N_LOOP) * PAR_DEV)[:, None, None]
    pair_base = (2 * jnp.arange(pair_count))[None, :, None]
    parents = device_base + pair_base + second
    return parents.reshape(LEAVES).astype(jnp.int32)


def draw_near_list(key, part):
    key = jax.random.fold_in(key, 19)
    key_scores, key_forced = jax.random.split(key, 2)
    span = 2 * REACH
    candidates = jnp.concatenate([jnp.arange(-REACH, 0), jnp.arange(1, REACH + 1)])
    scores = jax.random.randint(key_scores, (LEAVES, span), 0, span) * span + jnp.arange(span)[None, :]
    forced_leaf = jax.random.randint(key_forced, (N_LOOP,), 0, LEAF_DEV)
    leaf_numbers = jnp.arange(LEAVES)
    forced = leaf_numbers % LEAF_DEV == forced_leaf[leaf_numbers // LEAF_DEV]
    ends = (jnp.arange(span) == 0) | (jnp.arange(span) == span - 1)
    bonuses = (forced[:, None] & ends[None, :]).astype(jnp.int32) * (span * span)
    chosen = lax.top_k(scores + bonuses, NEAR - 1)[1]
    offsets = candidates[chosen]
    targets = leaf_numbers[:, None]
    others = jnp.mod(targets + offsets, LEAVES)
    return jnp.concatenate([targets, others], axis=1).astype(jnp.int32)


def block_scale(own_key, extent, cuts, low, top_value):
    def one(axis_at, shards_of):
        heights = jax.random.uniform(jax.random.fold_in(jax.random.fold_in(own_key, 6), axis_at), (shards_of,), jnp.float32, low / len(cuts), top_value / len(cuts))
        return jnp.repeat(jnp.exp(heights), extent[axis_at] // shards_of).reshape((-1,) + (1,) * (len(extent) - axis_at - 1))

    gain = one(*cuts[0])
    for cut in cuts[1:]:
        gain = gain * one(*cut)
    return gain


def bell_draw(own_key, extent, deviation, reach, cuts=(), held_as=jnp.bfloat16):
    array = jax.random.normal(own_key, extent, jnp.float32) * deviation
    if len(cuts) > 0:
        array = block_scale(own_key, extent, cuts, -0.22, 0.18) * array
    return jnp.clip(array, min=-reach, max=reach).astype(held_as)


def setup_inputs(seed: int = 0) -> dict:
    key_list = jax.random.split(jax.random.key(seed), 11)
    return {
        "signals": bell_draw(key_list[0], (R, POINTS), 1.0, 6.0, ((0, 2), (1, 128))),
        "near_tiles": bell_draw(key_list[1], (LEAVES, NEAR, B, B), (NEAR * B) ** -0.5, 0.125, ((0, 128), (1, 2))),
        "near_list": draw_near_list(jax.random.fold_in(key_list[10], 71), 0),
        "leaf_basis": bell_draw(key_list[3], (LEAVES, K, B), B ** -0.5, 0.375, ((0, 128),)),
        "transfer": bell_draw(key_list[4], (LEAVES, K, K), K ** -0.5, 0.75, ((0, 128),)),
        "parent": draw_parent(jax.random.fold_in(key_list[10], 71), 0),
        "coupling": bell_draw(key_list[6], (LEAVES, K, FAR * K), (FAR * K) ** -0.5, 0.15625, ((0, 128),)),
        "far_list": draw_far_list(jax.random.fold_in(key_list[10], 71), 0),
        "parent_coupling": bell_draw(key_list[8], (PARENTS, K, PFAR * K), (PFAR * K) ** -0.5, 0.1875, ((0, 128),)),
        "parent_far": draw_parent_far(jax.random.fold_in(key_list[10], 71), 0),
    }


def reference(signals, near_tiles, near_list, leaf_basis, transfer, parent, coupling, far_list, parent_coupling, parent_far):
    point_blocks = signals.reshape(R, LEAVES, B)
    coefficients = jnp.einsum("ckb,rcb->crk", leaf_basis.astype(jnp.float32), point_blocks.astype(jnp.float32)).astype(jnp.bfloat16)
    lifted = jnp.einsum("crk,cka->cra", coefficients.astype(jnp.float32), transfer.astype(jnp.float32))
    parent_coefficients = jax.ops.segment_sum(lifted, parent, num_segments=PARENTS).astype(jnp.bfloat16)
    parent_picked = jnp.take(parent_coefficients, parent_far, axis=0).astype(jnp.float32)
    parent_mats = parent_coupling.astype(jnp.float32).reshape(PARENTS, K, PFAR, K)
    parent_field = jnp.einsum("pjrk,pajk->pra", parent_picked, parent_mats).astype(jnp.bfloat16)

    def one_device(device_index):
        first_leaf = (device_index * LEAF_DEV).astype(jnp.int32)
        tile_set = lax.dynamic_slice_in_dim(near_tiles, first_leaf, LEAF_DEV, 0).astype(jnp.float32)
        near_rows = lax.dynamic_slice_in_dim(near_list, first_leaf, LEAF_DEV, 0)
        picked = jnp.take(point_blocks, near_rows, axis=1).astype(jnp.float32)
        near = jnp.einsum("tjab,rtjb->rta", tile_set, picked)
        far_rows = lax.dynamic_slice_in_dim(far_list, first_leaf, LEAF_DEV, 0)
        sources = jnp.take(coefficients, far_rows, axis=0).astype(jnp.float32)
        leaf_mats = lax.dynamic_slice_in_dim(coupling, first_leaf, LEAF_DEV, 0).astype(jnp.float32).reshape(LEAF_DEV, K, FAR, K)
        leaf_far = jnp.einsum("tjrk,tajk->tra", sources, leaf_mats)
        parent_rows = lax.dynamic_slice_in_dim(parent, first_leaf, LEAF_DEV, 0)
        down_in = jnp.take(parent_field, parent_rows, axis=0).astype(jnp.float32)
        transfer_rows = lax.dynamic_slice_in_dim(transfer, first_leaf, LEAF_DEV, 0).astype(jnp.float32)
        descended = jnp.einsum("cra,cka->crk", down_in, transfer_rows)
        combined = (leaf_far + descended).astype(jnp.bfloat16)
        basis_rows = lax.dynamic_slice_in_dim(leaf_basis, first_leaf, LEAF_DEV, 0).astype(jnp.float32)
        far_out = jnp.einsum("crk,ckb->rcb", combined.astype(jnp.float32), basis_rows)
        return (near + far_out).astype(jnp.bfloat16)

    pieces = lax.map(one_device, jnp.arange(N_LOOP, dtype=jnp.int32))
    return jnp.transpose(pieces, (1, 0, 2, 3)).reshape(R, POINTS)
```

```python
import functools

import jax
import jax.numpy as jnp
from jax import lax
from jax.experimental import pallas as pl
from jax.experimental.pallas import tpu as pltpu
from jax.sharding import PartitionSpec as P

Z, Y, X, C = 8, 4, 2, 2
PLANE = Y * X * C
MIB = 1 << 20
NT = (((1,), (1,)), ((), ()))
NN = (((1,), (0,)), ((), ()))


def loop_moves(target):
    moves = []
    for d in range(Z * PLANE):
        z, y, x, c = d // PLANE, d // (X * C) % Y, d // C % X, d % C
        z, y, x, c = target(z, y, x, c)
        moves.append((d, ((z % Z * Y + y % Y) * X + x) * C + c))
    return moves


def dot(a, b, dims):
    return lax.dot_general(a, b, dims, preferred_element_type=jnp.float32)


def pack(block):
    half = block.shape[0] // 2
    return jnp.concatenate([block[:half], block[half:]], axis=1)


def unpack(block):
    half = block.shape[1] // 2
    return jnp.concatenate([block[:, :half], block[:, half:]], axis=0)


def upward_kernel(place, parent, signals, basis, transfer, ids_col, ids_row, coef_out, pay_out, slot_out):
    leaf_count, rank, leaf_size = basis.shape
    sums = [jnp.zeros((signals.shape[0], rank), jnp.float32) for _ in range(2)]
    for c in range(leaf_count):
        block = signals[:, c * leaf_size : (c + 1) * leaf_size]
        coefs = dot(block, basis[c], NT).astype(jnp.bfloat16)
        coef_out[c] = pack(coefs)
        lifted = dot(coefs, transfer[c], NN)
        member = parent[c] - place[0] * 2
        sums = [s + jnp.where(member == i, lifted, 0.0) for i, s in enumerate(sums)]
    for i, s in enumerate(sums):
        pay_out[i * 32 : (i + 1) * 32] = pack(s.astype(jnp.bfloat16))
    count = ids_col.shape[0]
    owner_col, owner_row = ids_col[...] // leaf_count, ids_row[...] // leaf_count
    same = owner_col == owner_row
    at_col = lax.broadcasted_iota(jnp.int32, (count, count), 0)
    at_row = lax.broadcasted_iota(jnp.int32, (count, count), 1)
    seen_col = jnp.sum(jnp.where(same & (at_row < at_col), 1, 0), axis=1, keepdims=True)
    seen_row = jnp.sum(jnp.where(same & (at_col < at_row), 1, 0), axis=0, keepdims=True)
    hop = (owner_row // PLANE - place[0] // PLANE + Z) % Z
    slot_out[...] = owner_row % PLANE * (2 * Z) + hop * 2 + seen_row
    peers = lax.broadcasted_iota(jnp.int32, (count, Z * PLANE), 1)
    member_col = (ids_col[...] % leaf_count).astype(jnp.float32)
    rows = [
        jnp.sum(jnp.where((owner_col == peers) & (seen_col == i), member_col, 0.0), axis=0, keepdims=True)
        for i in range(2)
    ]
    rows.append(jnp.zeros((14, Z * PLANE), jnp.float32))
    pay_out[64:80] = jnp.concatenate(rows, axis=0).astype(jnp.bfloat16)


def upward(place, parent, signals, basis, transfer, far_list):
    leaf_count = basis.shape[0]
    smem = pl.BlockSpec(memory_space=pltpu.SMEM)
    vmem = pl.BlockSpec(memory_space=pltpu.VMEM)
    return pl.pallas_call(
        upward_kernel,
        out_shape=(
            jax.ShapeDtypeStruct((leaf_count, 32, 128), jnp.bfloat16),
            jax.ShapeDtypeStruct((80, 128), jnp.bfloat16),
            jax.ShapeDtypeStruct((1, far_list.size), jnp.int32),
        ),
        in_specs=[smem, smem, vmem, vmem, vmem, vmem, vmem],
        out_specs=(vmem, vmem, vmem),
        compiler_params=pltpu.CompilerParams(vmem_limit_bytes=16 * MIB),
        name="upward",
    )(place, parent, signals, basis, transfer, far_list.reshape(-1, 1), far_list.reshape(1, -1))


def select_kernel(place, wanted, *refs):
    planes, send = refs[:Z], refs[Z]
    step = pl.program_id(0)
    own = place[0] % PLANE
    first = place[0] // PLANE
    for i in range(send.shape[0]):
        peer = step * send.shape[0] + i
        dy = (peer // (X * C) - own // (X * C) + Y) % Y
        dx = (peer // C % X - own // C % X + X) % X
        dc = (peer % C - own % C + C) % C
        row = ((dc * Y + dy) * X + dx) * 2
        for hop in range(Z):
            lane = (first + hop) % Z * PLANE + own
            for k in range(2):
                send[i, hop * 2 + k] = planes[hop][wanted[row + k, lane]]


def select(place, wanted, planes):
    smem = pl.BlockSpec(memory_space=pltpu.SMEM)
    vmem = pl.BlockSpec(memory_space=pltpu.VMEM)
    per_step = 4
    return pl.pallas_call(
        select_kernel,
        grid=(PLANE // per_step,),
        out_shape=jax.ShapeDtypeStruct((PLANE, 2 * Z, 32, 128), jnp.bfloat16),
        in_specs=[smem, smem] + [vmem] * Z,
        out_specs=pl.BlockSpec((per_step, 2 * Z, 32, 128), lambda s: (s, 0, 0, 0)),
        compiler_params=pltpu.CompilerParams(vmem_limit_bytes=16 * MIB),
        name="select",
    )(place, wanted, *planes)


def near_kernel(place, near_list, both, before, after, tiles, own_out, other_out, extended):
    step = pl.program_id(0)
    rows, width = both.shape
    reach = before.shape[1]

    @pl.when(step == 0)
    def _():
        extended[:, :reach] = before[...]
        extended[:, reach : reach + width] = both[...]
        extended[:, reach + width :] = after[...]

    total = jnp.zeros((rows, tiles.shape[2]), jnp.float32)
    leaves = 8 * Z * PLANE
    for j in range(tiles.shape[1]):
        source = near_list[step, place[1] * tiles.shape[1] + j]
        at = (source - place[0] * 8 + 4 + leaves) % leaves
        block = extended[:, pl.ds(pl.multiple_of(at * 256, 256), 256)]
        total = total + dot(block, tiles[0, j], NT)
    own_out[...] = total[: rows // 2]
    other_out[...] = total[rows // 2 :].astype(jnp.bfloat16)


def near_field(place, near_list, both, before, after, tiles):
    smem = pl.BlockSpec(memory_space=pltpu.SMEM)
    vmem = pl.BlockSpec(memory_space=pltpu.VMEM)
    leaf_count, near_count, leaf_size, _ = tiles.shape
    rows, width = both.shape
    out_spec = pl.BlockSpec((rows // 2, leaf_size), lambda t: (0, t))
    return pl.pallas_call(
        near_kernel,
        grid=(leaf_count,),
        out_shape=(
            jax.ShapeDtypeStruct((rows // 2, width), jnp.float32),
            jax.ShapeDtypeStruct((rows // 2, width), jnp.bfloat16),
        ),
        in_specs=[smem, smem, vmem, vmem, vmem]
        + [pl.BlockSpec((1, near_count, leaf_size, leaf_size), lambda t: (t, 0, 0, 0))],
        out_specs=(out_spec, out_spec),
        scratch_shapes=[pltpu.VMEM((rows, 2 * width), jnp.bfloat16)],
        compiler_params=pltpu.CompilerParams(vmem_limit_bytes=16 * MIB),
        cost_estimate=pl.CostEstimate(flops=600_000_000, bytes_accessed=6_000_000, transcendentals=0),
        name="near_field",
    )(place, near_list, both, before, after, tiles)


def downward_kernel(
    place,
    parent,
    slots,
    parent_far,
    blocks,
    mine,
    theirs,
    parent_coupling,
    coupling,
    transfer,
    basis,
    near_own,
    near_in,
    out,
    fields,
    stacked,
):
    step = pl.program_id(0)
    rank = transfer.shape[1]
    half = blocks.shape[1]
    sources = coupling.shape[2] // rank

    @pl.when(step == 0)
    def _():
        own_plane = place[0] % PLANE
        for p in range(fields.shape[0]):
            total = jnp.zeros((2 * half, rank), jnp.float32)
            for j in range(parent_far.shape[1]):
                source = parent_far[p, j]
                device = source // 2
                dy = (device // (X * C) % Y - own_plane // (X * C) + Y) % Y
                dx = (device // C % X - own_plane // C % X + X) % X
                at = ((device // PLANE * Y + dy) * X + dx) * 2 + source % 2
                block = jnp.where(device % C == own_plane % C, mine[at], theirs[at])
                mat = parent_coupling[p, :, j * rank : (j + 1) * rank]
                total = total + dot(unpack(block), mat, NT)
            fields[p] = total.astype(jnp.bfloat16)

    for j in range(sources):
        block = blocks[slots[step, j]]
        stacked[:half, j * rank : (j + 1) * rank] = block[:, :rank]
        stacked[half:, j * rank : (j + 1) * rank] = block[:, rank:]
    leaf_far = dot(stacked[...], coupling[0], NT)
    field = fields[parent[step] - place[0] * 2]
    combined = (leaf_far + dot(field, transfer[0], NT)).astype(jnp.bfloat16)
    far_out = dot(combined, basis[0], NN)
    out[...] = (near_own[...] + near_in[...].astype(jnp.float32) + far_out).astype(jnp.bfloat16)


def downward(place, parent, slots, parent_far, blocks, mine, theirs, parent_coupling, coupling, transfer, basis, near_own, near_in):
    smem = pl.BlockSpec(memory_space=pltpu.SMEM)
    vmem = pl.BlockSpec(memory_space=pltpu.VMEM)
    leaf_count, rank, leaf_size = basis.shape
    rows = near_own.shape[0]

    def per_leaf(*shape):
        return pl.BlockSpec((1,) + shape, lambda t: (t, 0, 0))

    wide = pl.BlockSpec((rows, leaf_size), lambda t: (0, t))
    return pl.pallas_call(
        downward_kernel,
        grid=(leaf_count,),
        out_shape=jax.ShapeDtypeStruct(near_own.shape, jnp.bfloat16),
        in_specs=[smem] * 4
        + [vmem] * 4
        + [per_leaf(rank, coupling.shape[2]), per_leaf(rank, rank), per_leaf(rank, leaf_size), wide, wide],
        out_specs=wide,
        scratch_shapes=[
            pltpu.VMEM((parent_coupling.shape[0], rows, rank), jnp.bfloat16),
            pltpu.VMEM((rows, coupling.shape[2]), jnp.bfloat16),
        ],
        compiler_params=pltpu.CompilerParams(vmem_limit_bytes=24 * MIB),
        name="downward",
    )(place, parent, slots, parent_far, blocks, mine, theirs, parent_coupling, coupling, transfer, basis, near_own, near_in)


def shards(
    signals,
    near_tiles,
    near_list,
    leaf_basis,
    transfer,
    parent,
    coupling,
    far_list,
    parent_coupling,
    parent_far,
):
    columns, width = signals.shape
    place = jnp.stack([lax.axis_index("loop"), lax.axis_index("rhs")]).astype(jnp.int32)
    along = functools.partial(lax.ppermute, axis_name="loop")
    swap = functools.partial(lax.ppermute, axis_name="rhs", perm=[(0, 1), (1, 0)])
    z_down = loop_moves(lambda z, y, x, c: (z - 1, y, x, c))
    z_up = loop_moves(lambda z, y, x, c: (z + 1, y, x, c))
    x_swap = loop_moves(lambda z, y, x, c: (z, y, 1 - x, c))
    c_swap = loop_moves(lambda z, y, x, c: (z, y, x, 1 - c))
    z_groups = [[z * PLANE + p for z in range(Z)] for p in range(PLANE)]
    planes_of = [[z * PLANE + p for p in range(PLANE)] for z in range(Z)]

    other = swap(signals)
    coefs, payload, slots = upward(place, parent, signals, leaf_basis, transfer, far_list)

    planes = [coefs] + [None] * (Z - 1)
    for h in range(1, Z // 2 + 1):
        planes[h] = along(planes[h - 1], perm=z_down)
        if h < Z // 2:
            planes[Z - h] = along(planes[(Z - h + 1) % Z], perm=z_up)

    pair = jnp.stack([payload, along(payload, perm=x_swap)])
    quads = [pair] + [
        along(pair, perm=loop_moves(lambda z, y, x, c, dy=dy: (z, y - dy, x, c))) for dy in range(1, Y)
    ]
    plane_pay = jnp.stack(quads)
    wanted_mine = plane_pay[:, :, 64:80]
    wanted_theirs = along(wanted_mine, perm=c_swap)
    wanted = jnp.stack([wanted_mine, wanted_theirs])[:, :, :, :2].reshape(-1, Z * PLANE).astype(jnp.int32)
    parents_mine = lax.all_gather(
        plane_pay[:, :, :64].reshape(-1, 128), "loop", axis=0, tiled=True, axis_index_groups=z_groups
    )
    parents_theirs = along(parents_mine, perm=c_swap)
    parents_mine = parents_mine.reshape(-1, 32, 128)
    parents_theirs = parents_theirs.reshape(-1, 32, 128)

    both = jnp.concatenate([signals, other], axis=0)
    reach = width // 2
    count = Z * PLANE
    before = along(both[:, reach:], perm=[(i, (i + 1) % count) for i in range(count)])
    after = along(both[:, :reach], perm=[((i + 1) % count, i) for i in range(count)])
    near_own, near_other = near_field(place, near_list, both, before, after, near_tiles)
    near_in = swap(near_other)

    send = select(place, wanted, planes)
    blocks = lax.all_to_all(send, "loop", 0, 0, tiled=True, axis_index_groups=planes_of)
    return downward(
        place,
        parent,
        slots.reshape(far_list.shape),
        parent_far,
        blocks.reshape(-1, 32, 128),
        parents_mine,
        parents_theirs,
        parent_coupling,
        coupling,
        transfer,
        leaf_basis,
        near_own,
        near_in,
    )


def solution(mesh):
    in_specs = (
        P("rhs", "loop"),
        P("loop", "rhs", None, None),
        P("loop", None),
        P("loop", None, None),
        P("loop", None, None),
        P("loop"),
        P("loop", None, None),
        P("loop", None),
        P("loop", None, None),
        P("loop", None),
    )
    out_specs = P("rhs", "loop")
    return jax.shard_map(shards, mesh=mesh, in_specs=in_specs, out_specs=out_specs, check_vma=False)
```

```python
import functools

import jax
import jax.numpy as jnp
from jax import lax
from jax.experimental import pallas as pl
from jax.experimental.pallas import tpu as pltpu
from jax.sharding import PartitionSpec as P

Z, Y, X, C = 8, 4, 2, 2
PLANE = Y * X * C
MIB = 1 << 20
NT = (((1,), (1,)), ((), ()))
TN = (((0,), (0,)), ((), ()))
NN = (((1,), (0,)), ((), ()))


def loop_moves(target):
    moves = []
    for d in range(Z * PLANE):
        z, y, x, c = d // PLANE, d // (X * C) % Y, d // C % X, d % C
        z, y, x, c = target(z, y, x, c)
        moves.append((d, ((z % Z * Y + y % Y) * X + x) * C + c))
    return moves


def dot(a, b, dims):
    return lax.dot_general(a, b, dims, preferred_element_type=jnp.float32)


def pack(block):
    half = block.shape[0] // 2
    return jnp.concatenate([block[:half], block[half:]], axis=1)


def unpack(block):
    half = block.shape[1] // 2
    return [block, jnp.concatenate([block[:, half:], block[:, :half]], axis=1)]


def load(copies, sems):
    pending = [
        pltpu.make_async_copy(source, target, sems.at[i]) for i, (source, target) in enumerate(copies)
    ]
    for copy in pending:
        copy.start()
    return pending


SMEM_SPEC = pl.BlockSpec(memory_space=pltpu.SMEM)
VMEM_SPEC = pl.BlockSpec(memory_space=pltpu.VMEM)
ANY_SPEC = pl.BlockSpec(memory_space=pl.ANY)


def cost(flops, moved):
    return pl.CostEstimate(flops=flops, bytes_accessed=moved, transcendentals=0)


def tables_kernel(lists, own_row, wanted_out, slot_out):
    own = lax.axis_index("loop") % PLANE
    count = 2 * lists.shape[2]
    devices = jnp.concatenate([lists[0], lists[1]], axis=1)
    members = jnp.concatenate([lists[2], lists[3]], axis=1)
    flat = lax.broadcasted_iota(jnp.int32, devices.shape, 1)
    lane = lax.broadcasted_iota(jnp.int32, wanted_out.shape, 1)
    table = jnp.zeros(wanted_out.shape, jnp.int32)
    for z in range(Z):
        place = jnp.where(devices == z * PLANE + own, flat, count)
        lowest = jnp.min(place, axis=1, keepdims=True)
        place_two = jnp.where(place > lowest, place, count)
        second = jnp.min(place_two, axis=1, keepdims=True)
        for k, at in enumerate((lowest, second)):
            member = jnp.sum(jnp.where(flat == at, members, 0), axis=1, keepdims=True)
            table = jnp.where(lane == z * 2 + k, member, table)
    wanted_out[...] = table
    row = own_row[...]
    size = row.shape[1]
    at_col = lax.broadcasted_iota(jnp.int32, (size, size), 0)
    at_row = lax.broadcasted_iota(jnp.int32, (size, size), 1)
    column = jnp.sum(jnp.where(at_col == at_row, row, 0), axis=1, keepdims=True)
    earlier = jnp.where((column == row) & (at_col < at_row), 1, 0)
    seen = jnp.sum(earlier, axis=0, keepdims=True)
    slot_out[...] = row % PLANE * (2 * Z) + row // PLANE * 2 + seen


def tables(lists, own_row):
    return pl.pallas_call(
        tables_kernel,
        out_shape=(
            jax.ShapeDtypeStruct((PLANE, 128), jnp.int32),
            jax.ShapeDtypeStruct(own_row.shape, jnp.int32),
        ),
        in_specs=[VMEM_SPEC] * 2,
        out_specs=(VMEM_SPEC, VMEM_SPEC),
        compiler_params=pltpu.CompilerParams(vmem_limit_bytes=8 * MIB),
        cost_estimate=cost(2_000_000, 20_000),
        name="tables",
    )(lists, own_row)


def upward_kernel(
    parent, far_list, signals_in, basis_in, transfer_in, coef_out, pay_out, row_out, signals, basis, transfer, sems
):
    pending = load([(signals_in, signals), (basis_in, basis), (transfer_in, transfer)], sems)
    ids = far_list[...]
    row = jnp.concatenate([ids[t : t + 1] for t in range(ids.shape[0])], axis=1)
    row = jnp.concatenate([row, jnp.full((1, 256 - row.shape[1]), -8, jnp.int32)], axis=1)
    devices, members = row // ids.shape[0], row % ids.shape[0]
    row_out[...] = devices
    lists = [devices[:, :128], devices[:, 128:], members[:, :128], members[:, 128:], jnp.zeros((12, 128), jnp.int32)]
    pay_out[64:80] = jnp.concatenate(lists, axis=0).astype(jnp.float32).astype(jnp.bfloat16)
    for copy in pending:
        copy.wait()
    leaf_count, rank, leaf_size = basis.shape
    sums = [jnp.zeros((rank, signals.shape[0]), jnp.float32) for _ in range(2)]
    for c in range(leaf_count):
        block = signals[:, c * leaf_size : (c + 1) * leaf_size]
        coefs = dot(basis[c], block, NT).astype(jnp.bfloat16)
        packed = pack(coefs)
        for z in range(Z):
            coef_out[z, c] = packed
        lifted = dot(transfer[c], coefs, TN)
        member = parent[c] - lax.axis_index("loop") * 2
        sums = [s + jnp.where(member == i, lifted, 0.0) for i, s in enumerate(sums)]
    for i, s in enumerate(sums):
        pay_out[i * 32 : (i + 1) * 32] = pack(s.astype(jnp.bfloat16))


def upward(parent, far_list, signals, basis, transfer):
    leaf_count = basis.shape[0]
    return pl.pallas_call(
        upward_kernel,
        out_shape=(
            jax.ShapeDtypeStruct((Z, leaf_count, 32, 128), jnp.bfloat16),
            jax.ShapeDtypeStruct((80, 128), jnp.bfloat16),
            jax.ShapeDtypeStruct((1, 256), jnp.int32),
        ),
        in_specs=[SMEM_SPEC, VMEM_SPEC, ANY_SPEC, ANY_SPEC, ANY_SPEC],
        out_specs=(VMEM_SPEC,) * 3,
        scratch_shapes=[
            pltpu.VMEM(signals.shape, jnp.bfloat16),
            pltpu.VMEM(basis.shape, jnp.bfloat16),
            pltpu.VMEM(transfer.shape, jnp.bfloat16),
            pltpu.SemaphoreType.DMA((3,)),
        ],
        compiler_params=pltpu.CompilerParams(vmem_limit_bytes=56 * MIB),
        cost_estimate=cost(30_000_000, 700_000),
        name="upward",
    )(parent, far_list, signals, basis, transfer)


def select_kernel(wanted, planes, send):
    step = pl.program_id(0)
    own = lax.axis_index("loop") % PLANE
    for i in range(send.shape[0]):
        peer = step * send.shape[0] + i
        dy = jnp.bitwise_and(peer // (X * C) - own // (X * C) + Y, Y - 1)
        row = dy * (X * C) + jnp.bitwise_and(jnp.bitwise_xor(peer, own), X * C - 1)
        for slot in range(2 * Z):
            send[i, slot] = planes[slot // 2, wanted[row, slot]]


def select(wanted, planes):
    per_step = 4
    return pl.pallas_call(
        select_kernel,
        grid=(PLANE // per_step,),
        out_shape=jax.ShapeDtypeStruct((PLANE, 2 * Z, 32, 128), jnp.bfloat16),
        in_specs=[SMEM_SPEC, VMEM_SPEC],
        out_specs=pl.BlockSpec((per_step, 2 * Z, 32, 128), lambda s: (s, 0, 0, 0)),
        compiler_params=pltpu.CompilerParams(vmem_limit_bytes=8 * MIB),
        cost_estimate=cost(1_000_000, 2_500_000),
        name="select",
    )(wanted, planes)


def near_kernel(near_list, signals, other, before, after, tiles, own_out, other_out, extended, sems):
    half, width = signals.shape
    reach = before.shape[1]
    leaf_count, near_count, leaf_size, _ = tiles.shape
    pending = load(
        [
            (before, extended.at[:, :reach]),
            (signals, extended.at[:half, reach : reach + width]),
            (other, extended.at[half:, reach : reach + width]),
            (after, extended.at[:, reach + width :]),
        ],
        sems,
    )
    for copy in pending:
        copy.wait()
    loop, rhs = lax.axis_index("loop"), lax.axis_index("rhs")
    leaves = leaf_count * Z * PLANE
    for t in range(leaf_count):
        total = jnp.zeros((2 * half, leaf_size), jnp.float32)
        for j in range(near_count):
            source = near_list[t, rhs * near_count + j]
            at = (source - loop * leaf_count + leaf_count // 2 + leaves) % leaves
            block = extended[:, pl.ds(pl.multiple_of(at * leaf_size, leaf_size), leaf_size)]
            total = total + dot(block, tiles[t, j], NT)
        own_out[:, t * leaf_size : (t + 1) * leaf_size] = total[:half]
        other_out[:, t * leaf_size : (t + 1) * leaf_size] = total[half:].astype(jnp.bfloat16)


def near_field(near_list, signals, other, before, after, tiles):
    half, width = signals.shape
    return pl.pallas_call(
        near_kernel,
        out_shape=(
            jax.ShapeDtypeStruct((half, width), jnp.float32),
            jax.ShapeDtypeStruct((half, width), jnp.bfloat16),
        ),
        in_specs=[SMEM_SPEC, ANY_SPEC, ANY_SPEC, ANY_SPEC, ANY_SPEC, VMEM_SPEC],
        out_specs=(VMEM_SPEC, VMEM_SPEC),
        scratch_shapes=[
            pltpu.VMEM((2 * half, 2 * width), jnp.bfloat16),
            pltpu.SemaphoreType.DMA((4,)),
        ],
        compiler_params=pltpu.CompilerParams(vmem_limit_bytes=12 * MIB),
        cost_estimate=cost(600_000_000, 10_000_000),
        name="near_field",
    )(near_list, signals, other, before, after, tiles)


def fields_kernel(parent, parent_far, *refs):
    sources = refs[:9]
    coupling_in, transfer_in, out, parents, coupling, transfer, sems = refs[9:]
    copies = [(coupling_in, coupling), (transfer_in, transfer)]
    at = 0
    for ref in sources:
        copies.append((ref, parents.at[at : at + ref.shape[0]]))
        at += ref.shape[0]
    pending = load(copies, sems)
    for copy in pending:
        copy.wait()
    me = lax.axis_index("loop")
    own_plane = me % PLANE
    per = 2 * Y * X
    columns = out.shape[2]
    results = []
    for p in range(parent_far.shape[0]):
        stacked = []
        for j in range(parent_far.shape[1]):
            source = parent_far[p, j]
            device = source // 2
            hop = jnp.bitwise_and(device // PLANE - me // PLANE + Z, Z - 1)
            dy = jnp.bitwise_and(device // (X * C) - own_plane // (X * C) + Y, Y - 1)
            cross = jnp.bitwise_xor(device, own_plane)
            dx = jnp.bitwise_and(cross // C, X - 1)
            member = (dy * X + dx) * 2 + jnp.bitwise_and(source, 1)
            base = jnp.int32(0)
            for place, h in enumerate((0, 1, 7, 2, 3, 6, 5, 4)):
                base = jnp.where(hop == h, place * per, base)
            where = jnp.bitwise_and(cross, C - 1) * (Z * per) + base + member
            stacked += unpack(parents[where])
        field = dot(coupling[p], jnp.concatenate(stacked, axis=0), NN)
        results.append(field[:, :columns].astype(jnp.bfloat16))
    for c in range(transfer.shape[0]):
        field = jnp.where(parent[c] == me * 2, results[0], results[1])
        out[c] = dot(transfer[c], field, NN)


def fields(parent, parent_far, pieces, parent_coupling, transfer):
    return pl.pallas_call(
        fields_kernel,
        out_shape=jax.ShapeDtypeStruct(transfer.shape, jnp.float32),
        in_specs=[SMEM_SPEC] * 2 + [ANY_SPEC] * 11,
        out_specs=VMEM_SPEC,
        scratch_shapes=[
            pltpu.VMEM((2 * Z * Y * X * 2, 32, 128), jnp.bfloat16),
            pltpu.VMEM(parent_coupling.shape, jnp.bfloat16),
            pltpu.VMEM(transfer.shape, jnp.bfloat16),
            pltpu.SemaphoreType.DMA((11,)),
        ],
        compiler_params=pltpu.CompilerParams(vmem_limit_bytes=16 * MIB),
        cost_estimate=cost(50_000_000, 4_000_000),
        name="fields",
    )(parent, parent_far, *pieces, parent_coupling, transfer)


def downward_kernel(
    slots,
    blocks,
    coupling_in,
    descended_in,
    basis_in,
    near_own_in,
    near_in_in,
    out,
    coupling,
    descended,
    basis,
    near_own,
    near_in,
    sems,
):
    leaf_count, rank, leaf_size = basis.shape
    pending = load(
        [(coupling_in.at[c], coupling.at[c]) for c in range(leaf_count)]
        + [(descended_in, descended), (basis_in, basis), (near_own_in, near_own), (near_in_in, near_in)],
        sems,
    )
    sources = coupling.shape[2] // rank
    columns = out.shape[0]
    for c in range(leaf_count):
        stacked = []
        for j in range(sources):
            stacked += unpack(blocks[slots[0, c * sources + j]])
        pending[c].wait()
        if c == 0:
            for copy in pending[leaf_count:]:
                copy.wait()
        leaf_far = dot(coupling[c], jnp.concatenate(stacked, axis=0), NN)[:, :columns]
        combined = (leaf_far + descended[c]).astype(jnp.bfloat16)
        far_out = dot(combined, basis[c], TN)
        at = slice(c * leaf_size, (c + 1) * leaf_size)
        out[:, at] = (near_own[:, at] + near_in[:, at].astype(jnp.float32) + far_out).astype(jnp.bfloat16)


def downward(slots, blocks, coupling, descended, basis, near_own, near_in):
    arrays = (coupling, descended, basis, near_own, near_in)
    return pl.pallas_call(
        downward_kernel,
        out_shape=jax.ShapeDtypeStruct(near_own.shape, jnp.bfloat16),
        in_specs=[SMEM_SPEC, VMEM_SPEC] + [ANY_SPEC] * 5,
        out_specs=VMEM_SPEC,
        scratch_shapes=[pltpu.VMEM(a.shape, a.dtype) for a in arrays]
        + [pltpu.SemaphoreType.DMA((4 + coupling.shape[0],))],
        compiler_params=pltpu.CompilerParams(vmem_limit_bytes=60 * MIB),
        cost_estimate=cost(150_000_000, 6_000_000),
        name="downward",
    )(slots, blocks, *arrays)


def shards(
    signals,
    near_tiles,
    near_list,
    leaf_basis,
    transfer,
    parent,
    coupling,
    far_list,
    parent_coupling,
    parent_far,
):
    width = signals.shape[1]
    leaf_count = leaf_basis.shape[0]
    along = functools.partial(lax.ppermute, axis_name="loop")
    swap = functools.partial(lax.ppermute, axis_name="rhs", perm=[(0, 1), (1, 0)])
    x_swap = loop_moves(lambda z, y, x, c: (z, y, 1 - x, c))
    c_swap = loop_moves(lambda z, y, x, c: (z, y, x, 1 - c))
    columns_of = [[z * PLANE + p for z in range(Z)] for p in range(PLANE)]
    planes_of = [[z * PLANE + p for p in range(PLANE)] for z in range(Z)]

    other = swap(signals)
    coefs, payload, own_row = upward(parent, far_list, signals, leaf_basis, transfer)

    planes = lax.all_to_all(coefs, "loop", 0, 0, tiled=True, axis_index_groups=columns_of)
    pair = jnp.stack([payload, along(payload, perm=x_swap)])
    quads = jnp.stack(
        [pair]
        + [
            along(pair, perm=loop_moves(lambda z, y, x, c, dy=dy: (z, y - dy, x, c)))
            for dy in range(1, Y)
        ]
    )
    core_lists = quads[:, :, 64:68].reshape(Y * X, 4, 128)
    peer_lists = along(core_lists.reshape(-1, 128), perm=c_swap).reshape(Y * X, 4, 128)
    plane_lists = jnp.stack([core_lists, peer_lists], axis=1).reshape(PLANE, 4, 128).transpose(1, 0, 2)
    parents = quads[:, :, :64].reshape(-1, 32, 128)
    one_down = along(parents, perm=loop_moves(lambda z, y, x, c: (z - 1, y, x, c)))
    one_up = along(parents, perm=loop_moves(lambda z, y, x, c: (z + 1, y, x, c)))

    reach = width // 2
    count = Z * PLANE
    before = along(
        jnp.concatenate([signals[:, reach:], other[:, reach:]]), perm=[(i, (i + 1) % count) for i in range(count)]
    )
    after = along(
        jnp.concatenate([signals[:, :reach], other[:, :reach]]), perm=[((i + 1) % count, i) for i in range(count)]
    )
    plane_lists, before, after, one_down, one_up = lax.optimization_barrier(
        (plane_lists, before, after, one_down, one_up)
    )
    wanted, slots = tables(plane_lists.astype(jnp.int32), own_row)
    blocks = lax.all_to_all(
        select(wanted, planes), "loop", 0, 0, tiled=True, axis_index_groups=planes_of
    )

    far_down = along(jnp.concatenate([parents, one_down]), perm=loop_moves(lambda z, y, x, c: (z - 2, y, x, c)))
    far_up = along(jnp.concatenate([parents, one_up]), perm=loop_moves(lambda z, y, x, c: (z + 2, y, x, c)))
    near_own, near_other = near_field(near_list, signals, other, before, after, near_tiles)
    near_other, far_down, far_up = lax.optimization_barrier((near_other, far_down, far_up))
    near_in = swap(near_other)
    half = parents.shape[0] // 2
    last_down = along(far_down[2 * half : 3 * half], perm=loop_moves(lambda z, y, x, c: (z - 1, y, x, c)))
    last_up = along(far_up[3 * half :], perm=loop_moves(lambda z, y, x, c: (z + 1, y, x, c)))
    mine = [parents, one_down, one_up, far_down, far_up, last_down, last_up]
    theirs = [along(jnp.concatenate(part), perm=c_swap) for part in (mine[:5], mine[5:])]
    descended = fields(parent, parent_far, mine + theirs, parent_coupling, transfer)

    return downward(slots, blocks.reshape(-1, 32, 128), coupling, descended, leaf_basis, near_own, near_in)


def solution(mesh):
    in_specs = (
        P("rhs", "loop"),
        P("loop", "rhs", None, None),
        P("loop", None),
        P("loop", None, None),
        P("loop", None, None),
        P("loop"),
        P("loop", None, None),
        P("loop", None),
        P("loop", None, None),
        P("loop", None),
    )
    out_specs = P("rhs", "loop")
    return jax.shard_map(shards, mesh=mesh, in_specs=in_specs, out_specs=out_specs, check_vma=False)
```

```python
import functools

import jax
import jax.numpy as jnp
from jax import lax
from jax.experimental import pallas as pl
from jax.experimental.pallas import tpu as pltpu
from jax.sharding import PartitionSpec as P

Z, Y, X, C = 8, 4, 2, 2
PLANE = Y * X * C
MIB = 1 << 20
NT = (((1,), (1,)), ((), ()))
TN = (((0,), (0,)), ((), ()))
NN = (((1,), (0,)), ((), ()))


def loop_moves(target):
    moves = []
    for d in range(Z * PLANE):
        z, y, x, c = d // PLANE, d // (X * C) % Y, d // C % X, d % C
        z, y, x, c = target(z, y, x, c)
        moves.append((d, ((z % Z * Y + y % Y) * X + x) * C + c))
    return moves


def dot(a, b, dims):
    return lax.dot_general(a, b, dims, preferred_element_type=jnp.float32)


def pack(block):
    half = block.shape[0] // 2
    return jnp.concatenate([block[:half], block[half:]], axis=1)


def unpack(block):
    half = block.shape[1] // 2
    return [block, jnp.concatenate([block[:, half:], block[:, :half]], axis=1)]


def load(copies, sems):
    pending = [
        pltpu.make_async_copy(source, target, sems.at[i]) for i, (source, target) in enumerate(copies)
    ]
    for copy in pending:
        copy.start()
    return pending


SMEM_SPEC = pl.BlockSpec(memory_space=pltpu.SMEM)
VMEM_SPEC = pl.BlockSpec(memory_space=pltpu.VMEM)
ANY_SPEC = pl.BlockSpec(memory_space=pl.ANY)


def cost(flops, moved):
    return pl.CostEstimate(flops=flops, bytes_accessed=moved, transcendentals=0)


def tables_kernel(lists, own_row, wanted_out, slot_out):
    own = lax.axis_index("loop") % PLANE
    count = 2 * lists.shape[2]
    devices = jnp.concatenate([lists[0], lists[1]], axis=1)
    members = jnp.concatenate([lists[2], lists[3]], axis=1)
    flat = lax.broadcasted_iota(jnp.int32, devices.shape, 1)
    lane = lax.broadcasted_iota(jnp.int32, wanted_out.shape, 1)
    table = jnp.zeros(wanted_out.shape, jnp.int32)
    for z in range(Z):
        place = jnp.where(devices == z * PLANE + own, flat, count)
        lowest = jnp.min(place, axis=1, keepdims=True)
        place_two = jnp.where(place > lowest, place, count)
        second = jnp.min(place_two, axis=1, keepdims=True)
        for k, at in enumerate((lowest, second)):
            member = jnp.sum(jnp.where(flat == at, members, 0), axis=1, keepdims=True)
            table = jnp.where(lane == z * 2 + k, member, table)
    wanted_out[...] = table
    row = own_row[...]
    size = row.shape[1]
    at_col = lax.broadcasted_iota(jnp.int32, (size, size), 0)
    at_row = lax.broadcasted_iota(jnp.int32, (size, size), 1)
    column = jnp.sum(jnp.where(at_col == at_row, row, 0), axis=1, keepdims=True)
    earlier = jnp.where((column == row) & (at_col < at_row), 1, 0)
    seen = jnp.sum(earlier, axis=0, keepdims=True)
    slot_out[...] = row % PLANE * (2 * Z) + row // PLANE * 2 + seen


def tables(lists, own_row):
    return pl.pallas_call(
        tables_kernel,
        out_shape=(
            jax.ShapeDtypeStruct((PLANE, 128), jnp.int32),
            jax.ShapeDtypeStruct(own_row.shape, jnp.int32),
        ),
        in_specs=[VMEM_SPEC] * 2,
        out_specs=(VMEM_SPEC, VMEM_SPEC),
        compiler_params=pltpu.CompilerParams(vmem_limit_bytes=8 * MIB),
        cost_estimate=cost(2_000_000, 20_000),
        name="tables",
    )(lists, own_row)


def upward_kernel(
    parent, own_list, peer_list, signals_in, basis_in, transfer_in, coef_out, pay_out, row_out, signals, basis, transfer, sems
):
    pending = load([(signals_in, signals), (basis_in, basis), (transfer_in, transfer)], sems)
    lists = []
    for ref in (own_list, peer_list):
        ids = ref[...]
        row = jnp.concatenate([ids[t : t + 1] for t in range(ids.shape[0])], axis=1)
        row = jnp.concatenate([row, jnp.full((1, 256 - row.shape[1]), -8, jnp.int32)], axis=1)
        devices, members = row // ids.shape[0], row % ids.shape[0]
        lists += [devices[:, :128], devices[:, 128:], members[:, :128], members[:, 128:]]
        if ref is own_list:
            row_out[...] = devices
    lists.append(jnp.zeros((8, 128), jnp.int32))
    pay_out[64:80] = jnp.concatenate(lists, axis=0).astype(jnp.float32).astype(jnp.bfloat16)
    for copy in pending:
        copy.wait()
    leaf_count, rank, leaf_size = basis.shape
    sums = [jnp.zeros((rank, signals.shape[0]), jnp.float32) for _ in range(2)]
    for c in range(leaf_count):
        block = signals[:, c * leaf_size : (c + 1) * leaf_size]
        coefs = dot(basis[c], block, NT).astype(jnp.bfloat16)
        packed = pack(coefs)
        for z in range(Z):
            coef_out[z, c] = packed
        lifted = dot(transfer[c], coefs, TN)
        member = parent[c] - lax.axis_index("loop") * 2
        sums = [s + jnp.where(member == i, lifted, 0.0) for i, s in enumerate(sums)]
    for i, s in enumerate(sums):
        pay_out[i * 32 : (i + 1) * 32] = pack(s.astype(jnp.bfloat16))


def upward(parent, own_list, peer_list, signals, basis, transfer):
    leaf_count = basis.shape[0]
    return pl.pallas_call(
        upward_kernel,
        out_shape=(
            jax.ShapeDtypeStruct((Z, leaf_count, 32, 128), jnp.bfloat16),
            jax.ShapeDtypeStruct((80, 128), jnp.bfloat16),
            jax.ShapeDtypeStruct((1, 256), jnp.int32),
        ),
        in_specs=[SMEM_SPEC, VMEM_SPEC, VMEM_SPEC, ANY_SPEC, ANY_SPEC, ANY_SPEC],
        out_specs=(VMEM_SPEC,) * 3,
        scratch_shapes=[
            pltpu.VMEM(signals.shape, jnp.bfloat16),
            pltpu.VMEM(basis.shape, jnp.bfloat16),
            pltpu.VMEM(transfer.shape, jnp.bfloat16),
            pltpu.SemaphoreType.DMA((3,)),
        ],
        compiler_params=pltpu.CompilerParams(vmem_limit_bytes=56 * MIB),
        cost_estimate=cost(30_000_000, 700_000),
        name="upward",
    )(parent, own_list, peer_list, signals, basis, transfer)


def select_kernel(wanted, planes, send_out, send, sems):
    own = lax.axis_index("loop") % PLANE
    pending = []
    for peer in range(PLANE):
        dy = jnp.bitwise_and(peer // (X * C) - own // (X * C) + Y, Y - 1)
        row = dy * (X * C) + jnp.bitwise_and(jnp.bitwise_xor(peer, own), X * C - 1)
        for slot in range(2 * Z):
            send[peer, slot] = planes[slot // 2, wanted[row, slot]]
        pending.append(pltpu.make_async_copy(send.at[peer], send_out.at[peer], sems.at[peer]))
        pending[-1].start()
    for copy in pending:
        copy.wait()


def select(wanted, planes):
    shape = (PLANE, 2 * Z, 32, 128)
    return pl.pallas_call(
        select_kernel,
        out_shape=jax.ShapeDtypeStruct(shape, jnp.bfloat16),
        in_specs=[SMEM_SPEC, VMEM_SPEC],
        out_specs=ANY_SPEC,
        scratch_shapes=[pltpu.VMEM(shape, jnp.bfloat16), pltpu.SemaphoreType.DMA((PLANE,))],
        compiler_params=pltpu.CompilerParams(vmem_limit_bytes=8 * MIB),
        cost_estimate=cost(1_000_000, 2_500_000),
        name="select",
    )(wanted, planes)


def near_kernel(near_list, signals, other, before, after, tiles, own_out, other_out, extended, sems):
    half, width = signals.shape
    reach = before.shape[1]
    leaf_count, near_count, leaf_size, _ = tiles.shape
    pending = load(
        [
            (before, extended.at[:, :reach]),
            (signals, extended.at[:half, reach : reach + width]),
            (other, extended.at[half:, reach : reach + width]),
            (after, extended.at[:, reach + width :]),
        ],
        sems,
    )
    for copy in pending:
        copy.wait()
    loop, rhs = lax.axis_index("loop"), lax.axis_index("rhs")
    leaves = leaf_count * Z * PLANE
    for t in range(leaf_count):
        total = jnp.zeros((2 * half, leaf_size), jnp.float32)
        for j in range(near_count):
            source = near_list[t, rhs * near_count + j]
            at = (source - loop * leaf_count + leaf_count // 2 + leaves) % leaves
            block = extended[:, pl.ds(pl.multiple_of(at * leaf_size, leaf_size), leaf_size)]
            total = total + dot(block, tiles[t, j], NT)
        own_out[:, t * leaf_size : (t + 1) * leaf_size] = total[:half]
        other_out[:, t * leaf_size : (t + 1) * leaf_size] = total[half:].astype(jnp.bfloat16)


def near_field(near_list, signals, other, before, after, tiles):
    half, width = signals.shape
    return pl.pallas_call(
        near_kernel,
        out_shape=(
            jax.ShapeDtypeStruct((half, width), jnp.float32),
            jax.ShapeDtypeStruct((half, width), jnp.bfloat16),
        ),
        in_specs=[SMEM_SPEC, ANY_SPEC, ANY_SPEC, ANY_SPEC, ANY_SPEC, VMEM_SPEC],
        out_specs=(VMEM_SPEC, VMEM_SPEC),
        scratch_shapes=[
            pltpu.VMEM((2 * half, 2 * width), jnp.bfloat16),
            pltpu.SemaphoreType.DMA((4,)),
        ],
        compiler_params=pltpu.CompilerParams(vmem_limit_bytes=12 * MIB),
        cost_estimate=cost(600_000_000, 10_000_000),
        name="near_field",
    )(near_list, signals, other, before, after, tiles)


def fields_kernel(parent, parent_far, *refs):
    sources = refs[:11]
    coupling_in, transfer_in, out, parents, coupling, transfer, sems = refs[11:]
    copies = [(coupling_in, coupling), (transfer_in, transfer)]
    at = 0
    for ref in sources:
        copies.append((ref, parents.at[at : at + ref.shape[0]]))
        at += ref.shape[0]
    pending = load(copies, sems)
    for copy in pending:
        copy.wait()
    me = lax.axis_index("loop")
    own_plane = me % PLANE
    per = 2 * Y * X
    columns = out.shape[2]
    results = []
    for p in range(parent_far.shape[0]):
        stacked = []
        for j in range(parent_far.shape[1]):
            source = parent_far[p, j]
            device = source // 2
            hop = jnp.bitwise_and(device // PLANE - me // PLANE + Z, Z - 1)
            dy = jnp.bitwise_and(device // (X * C) - own_plane // (X * C) + Y, Y - 1)
            cross = jnp.bitwise_xor(device, own_plane)
            dx = jnp.bitwise_and(cross // C, X - 1)
            member = (dy * X + dx) * 2 + jnp.bitwise_and(source, 1)
            base = jnp.int32(0)
            for place, h in enumerate((0, 1, 7, 2, 6, 3, 5, 4)):
                base = jnp.where(hop == h, place * per, base)
            where = jnp.bitwise_and(cross, C - 1) * (Z * per) + base + member
            stacked += unpack(parents[where])
        field = dot(coupling[p], jnp.concatenate(stacked, axis=0), NN)
        results.append(field[:, :columns].astype(jnp.bfloat16))
    for c in range(transfer.shape[0]):
        field = jnp.where(parent[c] == me * 2, results[0], results[1])
        out[c] = dot(transfer[c], field, NN)


def fields(parent, parent_far, pieces, parent_coupling, transfer):
    return pl.pallas_call(
        fields_kernel,
        out_shape=jax.ShapeDtypeStruct(transfer.shape, jnp.float32),
        in_specs=[SMEM_SPEC] * 2 + [ANY_SPEC] * 13,
        out_specs=VMEM_SPEC,
        scratch_shapes=[
            pltpu.VMEM((2 * Z * Y * X * 2, 32, 128), jnp.bfloat16),
            pltpu.VMEM(parent_coupling.shape, jnp.bfloat16),
            pltpu.VMEM(transfer.shape, jnp.bfloat16),
            pltpu.SemaphoreType.DMA((13,)),
        ],
        compiler_params=pltpu.CompilerParams(vmem_limit_bytes=16 * MIB),
        cost_estimate=cost(50_000_000, 4_000_000),
        name="fields",
    )(parent, parent_far, *pieces, parent_coupling, transfer)


def downward_kernel(
    slots,
    blocks_in,
    near_in_in,
    coupling_in,
    descended_in,
    basis_in,
    near_own_in,
    out_hbm,
    blocks,
    near_in,
    coupling,
    descended,
    basis,
    near_own,
    stacked,
    out,
    sems,
    out_sems,
):
    leaf_count, rank, leaf_size = basis.shape
    part = blocks.shape[0] // 8
    pending = load(
        [(blocks_in.at[pl.ds(i * part, part)], blocks.at[pl.ds(i * part, part)]) for i in range(8)]
        + [(coupling_in.at[c], coupling.at[c]) for c in range(leaf_count)]
        + [(descended_in, descended), (basis_in, basis), (near_own_in, near_own), (near_in_in, near_in)],
        sems,
    )
    for copy in pending[:8]:
        copy.wait()
    sources = coupling.shape[2] // rank
    columns = out.shape[0]
    for c in range(leaf_count):
        for j in range(sources):
            pieces = jnp.concatenate(unpack(blocks[slots[0, c * sources + j]]), axis=0)
            stacked[c, j * rank : (j + 1) * rank] = pieces
    for copy in pending[8:]:
        copy.wait()
    written = []
    for c in range(leaf_count):
        leaf_far = dot(coupling[c], stacked[c], NN)[:, :columns]
        combined = (leaf_far + descended[c]).astype(jnp.bfloat16)
        far_out = dot(combined, basis[c], TN)
        at = pl.ds(c * leaf_size, leaf_size)
        out[:, at] = (near_own[:, at] + near_in[:, at].astype(jnp.float32) + far_out).astype(jnp.bfloat16)
        written.append(pltpu.make_async_copy(out.at[:, at], out_hbm.at[:, at], out_sems.at[c]))
        written[-1].start()
    for copy in written:
        copy.wait()


def downward(slots, blocks, coupling, descended, basis, near_own, near_in):
    arrays = (blocks, near_in, coupling, descended, basis, near_own)
    leaf_count = basis.shape[0]
    return pl.pallas_call(
        downward_kernel,
        out_shape=jax.ShapeDtypeStruct(near_own.shape, jnp.bfloat16),
        in_specs=[SMEM_SPEC] + [ANY_SPEC] * 6,
        out_specs=ANY_SPEC,
        scratch_shapes=[pltpu.VMEM(a.shape, a.dtype) for a in arrays]
        + [
            pltpu.VMEM((leaf_count, coupling.shape[2], 128), jnp.bfloat16),
            pltpu.VMEM(near_own.shape, jnp.bfloat16),
            pltpu.SemaphoreType.DMA((12 + leaf_count,)),
            pltpu.SemaphoreType.DMA((leaf_count,)),
        ],
        compiler_params=pltpu.CompilerParams(vmem_limit_bytes=62 * MIB),
        cost_estimate=cost(150_000_000, 6_000_000),
        name="downward",
    )(slots, *arrays)


def shards(
    signals,
    near_tiles,
    near_list,
    leaf_basis,
    transfer,
    parent,
    coupling,
    far_list,
    parent_coupling,
    parent_far,
):
    width = signals.shape[1]
    leaf_count = leaf_basis.shape[0]
    along = functools.partial(lax.ppermute, axis_name="loop")
    swap = functools.partial(lax.ppermute, axis_name="rhs", perm=[(0, 1), (1, 0)])
    x_swap = loop_moves(lambda z, y, x, c: (z, y, 1 - x, c))
    c_swap = loop_moves(lambda z, y, x, c: (z, y, x, 1 - c))
    columns_of = [[z * PLANE + p for z in range(Z)] for p in range(PLANE)]
    planes_of = [[z * PLANE + p for p in range(PLANE)] for z in range(Z)]

    other = swap(signals)
    peer_list = along(far_list, perm=c_swap)
    coefs, payload, own_row = upward(parent, far_list, peer_list, signals, leaf_basis, transfer)

    planes = lax.all_to_all(coefs, "loop", 0, 0, tiled=True, axis_index_groups=columns_of)
    pair = jnp.stack([payload, along(payload, perm=x_swap)])
    quads = jnp.stack(
        [pair]
        + [
            along(pair, perm=loop_moves(lambda z, y, x, c, dy=dy: (z, y - dy, x, c)))
            for dy in range(1, Y)
        ]
    )
    plane_lists = quads[:, :, 64:72].reshape(PLANE, 4, 128).transpose(1, 0, 2)
    parents = quads[:, :, :64].reshape(-1, 32, 128)
    down = functools.partial(along, perm=loop_moves(lambda z, y, x, c: (z - 1, y, x, c)))
    up = functools.partial(along, perm=loop_moves(lambda z, y, x, c: (z + 1, y, x, c)))
    one_down, one_up = down(parents), up(parents)

    reach = width // 2
    count = Z * PLANE
    before = along(
        jnp.concatenate([signals[:, reach:], other[:, reach:]]), perm=[(i, (i + 1) % count) for i in range(count)]
    )
    after = along(
        jnp.concatenate([signals[:, :reach], other[:, :reach]]), perm=[((i + 1) % count, i) for i in range(count)]
    )
    wanted, slots = tables(plane_lists.astype(jnp.int32), own_row)
    send, before, after, one_down, one_up = lax.optimization_barrier(
        (select(wanted, planes), before, after, one_down, one_up)
    )
    blocks = lax.all_to_all(send, "loop", 0, 0, tiled=True, axis_index_groups=planes_of)

    two_down, two_up = down(one_down), up(one_up)
    near_own, near_other = near_field(near_list, signals, other, before, after, near_tiles)
    near_in = swap(near_other)
    _, two_down, two_up = lax.optimization_barrier((near_other, two_down, two_up))
    three_down, three_up = down(two_down), up(two_up)
    half = parents.shape[0] // 2
    four_down, four_up = down(three_down[:half]), up(three_up[half:])
    mine = [parents, one_down, one_up, two_down, two_up, three_down, three_up, four_down, four_up]
    theirs = [along(jnp.concatenate(part), perm=c_swap) for part in (mine[:7], mine[7:])]
    descended = fields(parent, parent_far, mine + theirs, parent_coupling, transfer)

    return downward(slots, blocks.reshape(-1, 32, 128), coupling, descended, leaf_basis, near_own, near_in)


def solution(mesh):
    in_specs = (
        P("rhs", "loop"),
        P("loop", "rhs", None, None),
        P("loop", None),
        P("loop", None, None),
        P("loop", None, None),
        P("loop"),
        P("loop", None, None),
        P("loop", None),
        P("loop", None, None),
        P("loop", None),
    )
    out_specs = P("rhs", "loop")
    return jax.shard_map(shards, mesh=mesh, in_specs=in_specs, out_specs=out_specs, check_vma=False)
```

```python
import functools

import jax
import jax.numpy as jnp
from jax import lax
from jax.experimental import pallas as pl
from jax.experimental.pallas import tpu as pltpu
from jax.sharding import PartitionSpec as P

Z, Y, X, C = 8, 4, 2, 2
PLANE = Y * X * C
MIB = 1 << 20
NT = (((1,), (1,)), ((), ()))
TN = (((0,), (0,)), ((), ()))
NN = (((1,), (0,)), ((), ()))


def loop_moves(target):
    moves = []
    for d in range(Z * PLANE):
        z, y, x, c = d // PLANE, d // (X * C) % Y, d // C % X, d % C
        z, y, x, c = target(z, y, x, c)
        moves.append((d, ((z % Z * Y + y % Y) * X + x) * C + c))
    return moves


def dot(a, b, dims):
    return lax.dot_general(a, b, dims, preferred_element_type=jnp.float32)


def pack(block):
    half = block.shape[0] // 2
    return jnp.concatenate([block[:half], block[half:]], axis=1)


def unpack(block):
    half = block.shape[1] // 2
    return [block, jnp.concatenate([block[:, half:], block[:, :half]], axis=1)]


def load(copies, sems):
    pending = [
        pltpu.make_async_copy(source, target, sems.at[i]) for i, (source, target) in enumerate(copies)
    ]
    for copy in pending:
        copy.start()
    return pending


SMEM_SPEC = pl.BlockSpec(memory_space=pltpu.SMEM)
VMEM_SPEC = pl.BlockSpec(memory_space=pltpu.VMEM)
ANY_SPEC = pl.BlockSpec(memory_space=pl.ANY)


def cost(flops, moved):
    return pl.CostEstimate(flops=flops, bytes_accessed=moved, transcendentals=0)


def tables_kernel(lists, wanted_out):
    own = lax.axis_index("loop") % PLANE
    count = 2 * lists.shape[2]
    devices = jnp.concatenate([lists[0], lists[1]], axis=1)
    members = jnp.concatenate([lists[2], lists[3]], axis=1)
    flat = lax.broadcasted_iota(jnp.int32, devices.shape, 1)
    lane = lax.broadcasted_iota(jnp.int32, wanted_out.shape, 1)
    table = jnp.zeros(wanted_out.shape, jnp.int32)
    for z in range(Z):
        place = jnp.where(devices == z * PLANE + own, flat, count)
        lowest = jnp.min(place, axis=1, keepdims=True)
        place_two = jnp.where(place > lowest, place, count)
        second = jnp.min(place_two, axis=1, keepdims=True)
        for k, at in enumerate((lowest, second)):
            member = jnp.sum(jnp.where(flat == at, members, 0), axis=1, keepdims=True)
            table = jnp.where(lane == z * 2 + k, member, table)
    wanted_out[...] = table


def tables(lists):
    return pl.pallas_call(
        tables_kernel,
        out_shape=jax.ShapeDtypeStruct((PLANE, 128), jnp.int32),
        in_specs=[VMEM_SPEC],
        out_specs=VMEM_SPEC,
        compiler_params=pltpu.CompilerParams(vmem_limit_bytes=8 * MIB),
        cost_estimate=cost(2_000_000, 20_000),
        name="tables",
    )(lists)


def upward_kernel(
    parent, own_list, peer_list, signals_in, basis_in, transfer_in, coef_out, pay_out, row_out, signals, basis, transfer, sems
):
    pending = load([(signals_in, signals), (basis_in, basis), (transfer_in, transfer)], sems)
    lists = []
    for ref in (own_list, peer_list):
        ids = ref[...]
        row = jnp.concatenate([ids[t : t + 1] for t in range(ids.shape[0])], axis=1)
        row = jnp.concatenate([row, jnp.full((1, 256 - row.shape[1]), -8, jnp.int32)], axis=1)
        devices, members = row // ids.shape[0], row % ids.shape[0]
        lists += [devices[:, :128], devices[:, 128:], members[:, :128], members[:, 128:]]
        if ref is own_list:
            row_out[...] = devices
    lists.append(jnp.zeros((8, 128), jnp.int32))
    pay_out[64:80] = jnp.concatenate(lists, axis=0).astype(jnp.float32).astype(jnp.bfloat16)
    for copy in pending:
        copy.wait()
    leaf_count, rank, leaf_size = basis.shape
    sums = [jnp.zeros((rank, signals.shape[0]), jnp.float32) for _ in range(2)]
    for c in range(leaf_count):
        block = signals[:, c * leaf_size : (c + 1) * leaf_size]
        coefs = dot(basis[c], block, NT).astype(jnp.bfloat16)
        packed = pack(coefs)
        for z in range(Z):
            coef_out[z, c] = packed
        lifted = dot(transfer[c], coefs, TN)
        member = parent[c] - lax.axis_index("loop") * 2
        sums = [s + jnp.where(member == i, lifted, 0.0) for i, s in enumerate(sums)]
    for i, s in enumerate(sums):
        pay_out[i * 32 : (i + 1) * 32] = pack(s.astype(jnp.bfloat16))


def upward(parent, own_list, peer_list, signals, basis, transfer):
    leaf_count = basis.shape[0]
    return pl.pallas_call(
        upward_kernel,
        out_shape=(
            jax.ShapeDtypeStruct((Z, leaf_count, 32, 128), jnp.bfloat16),
            jax.ShapeDtypeStruct((80, 128), jnp.bfloat16),
            jax.ShapeDtypeStruct((1, 256), jnp.int32),
        ),
        in_specs=[SMEM_SPEC, VMEM_SPEC, VMEM_SPEC, ANY_SPEC, ANY_SPEC, ANY_SPEC],
        out_specs=(VMEM_SPEC,) * 3,
        scratch_shapes=[
            pltpu.VMEM(signals.shape, jnp.bfloat16),
            pltpu.VMEM(basis.shape, jnp.bfloat16),
            pltpu.VMEM(transfer.shape, jnp.bfloat16),
            pltpu.SemaphoreType.DMA((3,)),
        ],
        compiler_params=pltpu.CompilerParams(vmem_limit_bytes=56 * MIB),
        cost_estimate=cost(30_000_000, 700_000),
        name="upward",
    )(parent, own_list, peer_list, signals, basis, transfer)


def select_kernel(wanted, planes, send_out, send, sems):
    own = lax.axis_index("loop") % PLANE
    pending = []
    for peer in range(PLANE):
        dy = jnp.bitwise_and(peer // (X * C) - own // (X * C) + Y, Y - 1)
        row = dy * (X * C) + jnp.bitwise_and(jnp.bitwise_xor(peer, own), X * C - 1)
        for slot in range(2 * Z):
            send[peer, slot] = planes[slot // 2, wanted[row, slot]]
        pending.append(pltpu.make_async_copy(send.at[peer], send_out.at[peer], sems.at[peer]))
        pending[-1].start()
    for copy in pending:
        copy.wait()


def select(wanted, planes):
    shape = (PLANE, 2 * Z, 32, 128)
    return pl.pallas_call(
        select_kernel,
        out_shape=jax.ShapeDtypeStruct(shape, jnp.bfloat16),
        in_specs=[SMEM_SPEC, VMEM_SPEC],
        out_specs=ANY_SPEC,
        scratch_shapes=[pltpu.VMEM(shape, jnp.bfloat16), pltpu.SemaphoreType.DMA((PLANE,))],
        compiler_params=pltpu.CompilerParams(vmem_limit_bytes=8 * MIB),
        cost_estimate=cost(1_000_000, 2_500_000),
        name="select",
    )(wanted, planes)


def near_kernel(
    near_list, own_row, signals, other, before, after, tiles, own_out, other_out, slot_out, extended, sems
):
    half, width = signals.shape
    reach = before.shape[1]
    leaf_count, near_count, leaf_size, _ = tiles.shape
    pending = load(
        [
            (before, extended.at[:, :reach]),
            (signals, extended.at[:half, reach : reach + width]),
            (other, extended.at[half:, reach : reach + width]),
            (after, extended.at[:, reach + width :]),
        ],
        sems,
    )
    for copy in pending:
        copy.wait()
    row = own_row[...]
    size = row.shape[1]
    at_col = lax.broadcasted_iota(jnp.int32, (size, size), 0)
    at_row = lax.broadcasted_iota(jnp.int32, (size, size), 1)
    column = jnp.sum(jnp.where(at_col == at_row, row, 0), axis=1, keepdims=True)
    earlier = jnp.where((column == row) & (at_col < at_row), 1, 0)
    seen = jnp.sum(earlier, axis=0, keepdims=True)
    slot_out[...] = row % PLANE * (2 * Z) + row // PLANE * 2 + seen
    loop, rhs = lax.axis_index("loop"), lax.axis_index("rhs")
    leaves = leaf_count * Z * PLANE
    for t in range(leaf_count):
        total = jnp.zeros((2 * half, leaf_size), jnp.float32)
        for j in range(near_count):
            source = near_list[t, rhs * near_count + j]
            at = (source - loop * leaf_count + leaf_count // 2 + leaves) % leaves
            block = extended[:, pl.ds(pl.multiple_of(at * leaf_size, leaf_size), leaf_size)]
            total = total + dot(block, tiles[t, j], NT)
        own_out[:, t * leaf_size : (t + 1) * leaf_size] = total[:half]
        other_out[:, t * leaf_size : (t + 1) * leaf_size] = total[half:].astype(jnp.bfloat16)


def near_field(near_list, own_row, signals, other, before, after, tiles):
    half, width = signals.shape
    return pl.pallas_call(
        near_kernel,
        out_shape=(
            jax.ShapeDtypeStruct((half, width), jnp.float32),
            jax.ShapeDtypeStruct((half, width), jnp.bfloat16),
            jax.ShapeDtypeStruct(own_row.shape, jnp.int32),
        ),
        in_specs=[SMEM_SPEC, VMEM_SPEC, ANY_SPEC, ANY_SPEC, ANY_SPEC, ANY_SPEC, VMEM_SPEC],
        out_specs=(VMEM_SPEC,) * 3,
        scratch_shapes=[
            pltpu.VMEM((2 * half, 2 * width), jnp.bfloat16),
            pltpu.SemaphoreType.DMA((4,)),
        ],
        compiler_params=pltpu.CompilerParams(vmem_limit_bytes=12 * MIB),
        cost_estimate=cost(600_000_000, 10_000_000),
        name="near_field",
    )(near_list, own_row, signals, other, before, after, tiles)


def fields_kernel(parent, parent_far, *refs):
    sources = refs[:11]
    coupling, transfer, out, parents = refs[11:]
    at = 0
    for ref in sources:
        parents[at : at + ref.shape[0]] = ref[...]
        at += ref.shape[0]
    me = lax.axis_index("loop")
    own_plane = me % PLANE
    per = 2 * Y * X
    columns = out.shape[2]
    results = []
    for p in range(parent_far.shape[0]):
        stacked = []
        for j in range(parent_far.shape[1]):
            source = parent_far[p, j]
            device = source // 2
            hop = jnp.bitwise_and(device // PLANE - me // PLANE + Z, Z - 1)
            dy = jnp.bitwise_and(device // (X * C) - own_plane // (X * C) + Y, Y - 1)
            cross = jnp.bitwise_xor(device, own_plane)
            dx = jnp.bitwise_and(cross // C, X - 1)
            member = (dy * X + dx) * 2 + jnp.bitwise_and(source, 1)
            base = jnp.int32(0)
            for place, h in enumerate((0, 1, 7, 2, 6, 3, 5, 4)):
                base = jnp.where(hop == h, place * per, base)
            where = jnp.bitwise_and(cross, C - 1) * (Z * per) + base + member
            stacked += unpack(parents[where])
        field = dot(coupling[p], jnp.concatenate(stacked, axis=0), NN)
        results.append(field[:, :columns].astype(jnp.bfloat16))
    for c in range(transfer.shape[0]):
        field = jnp.where(parent[c] == me * 2, results[0], results[1])
        out[c] = dot(transfer[c], field, NN)


def fields(parent, parent_far, pieces, parent_coupling, transfer):
    return pl.pallas_call(
        fields_kernel,
        out_shape=jax.ShapeDtypeStruct(transfer.shape, jnp.float32),
        in_specs=[SMEM_SPEC] * 2 + [VMEM_SPEC] * 13,
        out_specs=VMEM_SPEC,
        scratch_shapes=[pltpu.VMEM((2 * Z * Y * X * 2, 32, 128), jnp.bfloat16)],
        compiler_params=pltpu.CompilerParams(vmem_limit_bytes=16 * MIB),
        cost_estimate=cost(50_000_000, 4_000_000),
        name="fields",
    )(parent, parent_far, *pieces, parent_coupling, transfer)


def downward_kernel(
    slots,
    blocks_in,
    coupling_in,
    descended_in,
    basis_in,
    near_own_in,
    out_hbm,
    blocks,
    coupling,
    descended,
    basis,
    near_own,
    stacked,
    out,
    sems,
    out_sems,
):
    leaf_count, rank, leaf_size = basis.shape
    part = blocks.shape[0] // 8
    pending = load(
        [(blocks_in.at[pl.ds(i * part, part)], blocks.at[pl.ds(i * part, part)]) for i in range(8)]
        + [(coupling_in.at[c], coupling.at[c]) for c in range(leaf_count)]
        + [(descended_in, descended), (basis_in, basis), (near_own_in, near_own)],
        sems,
    )
    for copy in pending[:8]:
        copy.wait()
    sources = coupling.shape[2] // rank
    columns = out.shape[0]
    for c in range(leaf_count):
        for j in range(sources):
            pieces = jnp.concatenate(unpack(blocks[slots[0, c * sources + j]]), axis=0)
            stacked[c, j * rank : (j + 1) * rank] = pieces
    for copy in pending[8:]:
        copy.wait()
    written = []
    for c in range(leaf_count):
        leaf_far = dot(coupling[c], stacked[c], NN)[:, :columns]
        combined = (leaf_far + descended[c]).astype(jnp.bfloat16)
        far_out = dot(combined, basis[c], TN)
        at = pl.ds(c * leaf_size, leaf_size)
        out[:, at] = near_own[:, at] + far_out
        written.append(pltpu.make_async_copy(out.at[:, at], out_hbm.at[:, at], out_sems.at[c]))
        written[-1].start()
    for copy in written:
        copy.wait()


def downward(slots, blocks, coupling, descended, basis, near_own):
    arrays = (blocks, coupling, descended, basis, near_own)
    leaf_count = basis.shape[0]
    return pl.pallas_call(
        downward_kernel,
        out_shape=jax.ShapeDtypeStruct(near_own.shape, jnp.float32),
        in_specs=[SMEM_SPEC] + [ANY_SPEC] * 5,
        out_specs=ANY_SPEC,
        scratch_shapes=[pltpu.VMEM(a.shape, a.dtype) for a in arrays]
        + [
            pltpu.VMEM((leaf_count, coupling.shape[2], 128), jnp.bfloat16),
            pltpu.VMEM(near_own.shape, jnp.float32),
            pltpu.SemaphoreType.DMA((11 + leaf_count,)),
            pltpu.SemaphoreType.DMA((leaf_count,)),
        ],
        compiler_params=pltpu.CompilerParams(vmem_limit_bytes=62 * MIB),
        cost_estimate=cost(150_000_000, 6_000_000),
        name="downward",
    )(slots, *arrays)


def shards(
    signals,
    near_tiles,
    near_list,
    leaf_basis,
    transfer,
    parent,
    coupling,
    far_list,
    parent_coupling,
    parent_far,
):
    width = signals.shape[1]
    leaf_count = leaf_basis.shape[0]
    along = functools.partial(lax.ppermute, axis_name="loop")
    swap = functools.partial(lax.ppermute, axis_name="rhs", perm=[(0, 1), (1, 0)])
    x_swap = loop_moves(lambda z, y, x, c: (z, y, 1 - x, c))
    c_swap = loop_moves(lambda z, y, x, c: (z, y, x, 1 - c))
    columns_of = [[z * PLANE + p for z in range(Z)] for p in range(PLANE)]
    planes_of = [[z * PLANE + p for p in range(PLANE)] for z in range(Z)]

    other = swap(signals)
    peer_list = along(far_list, perm=c_swap)
    coefs, payload, own_row = upward(parent, far_list, peer_list, signals, leaf_basis, transfer)

    planes = lax.all_to_all(coefs, "loop", 0, 0, tiled=True, axis_index_groups=columns_of)
    pair = jnp.stack([payload, along(payload, perm=x_swap)])
    quads = jnp.stack(
        [pair]
        + [
            along(pair, perm=loop_moves(lambda z, y, x, c, dy=dy: (z, y - dy, x, c)))
            for dy in range(1, Y)
        ]
    )
    plane_lists = quads[:, :, 64:72].reshape(PLANE, 4, 128).transpose(1, 0, 2)
    parents = quads[:, :, :64].reshape(-1, 32, 128)
    down = functools.partial(along, perm=loop_moves(lambda z, y, x, c: (z - 1, y, x, c)))
    up = functools.partial(along, perm=loop_moves(lambda z, y, x, c: (z + 1, y, x, c)))
    one_down, one_up = down(parents), up(parents)

    reach = width // 2
    count = Z * PLANE
    before = along(
        jnp.concatenate([signals[:, reach:], other[:, reach:]]), perm=[(i, (i + 1) % count) for i in range(count)]
    )
    after = along(
        jnp.concatenate([signals[:, :reach], other[:, :reach]]), perm=[((i + 1) % count, i) for i in range(count)]
    )
    wanted = tables(plane_lists.astype(jnp.int32))
    send, before, after, one_down, one_up = lax.optimization_barrier(
        (select(wanted, planes), before, after, one_down, one_up)
    )
    blocks = lax.all_to_all(send, "loop", 0, 0, tiled=True, axis_index_groups=planes_of)

    two_down, two_up = down(one_down), up(one_up)
    near_own, near_other, slots = near_field(near_list, own_row, signals, other, before, after, near_tiles)
    near_in = swap(near_other)
    _, two_down, two_up = lax.optimization_barrier((near_other, two_down, two_up))
    three_down, three_up = down(two_down), up(two_up)
    half = parents.shape[0] // 2
    four_down, four_up = down(three_down[:half]), up(three_up[half:])
    mine = [parents, one_down, one_up, two_down, two_up, three_down, three_up, four_down, four_up]
    theirs = [along(jnp.concatenate(part), perm=c_swap) for part in (mine[:7], mine[7:])]
    descended = fields(parent, parent_far, mine + theirs, parent_coupling, transfer)

    partial = downward(slots, blocks.reshape(-1, 32, 128), coupling, descended, leaf_basis, near_own)
    return (partial + near_in.astype(jnp.float32)).astype(jnp.bfloat16)


def solution(mesh):
    in_specs = (
        P("rhs", "loop"),
        P("loop", "rhs", None, None),
        P("loop", None),
        P("loop", None, None),
        P("loop", None, None),
        P("loop"),
        P("loop", None, None),
        P("loop", None),
        P("loop", None, None),
        P("loop", None),
    )
    out_specs = P("rhs", "loop")
    return jax.shard_map(shards, mesh=mesh, in_specs=in_specs, out_specs=out_specs, check_vma=False)
```

```python
import functools

import jax
import jax.numpy as jnp
from jax import lax
from jax.experimental import pallas as pl
from jax.experimental.pallas import tpu as pltpu
from jax.sharding import PartitionSpec as P

Z, Y, X, C = 8, 4, 2, 2
PLANE = Y * X * C
MIB = 1 << 20
NT = (((1,), (1,)), ((), ()))
TN = (((0,), (0,)), ((), ()))
NN = (((1,), (0,)), ((), ()))


def loop_moves(target):
    moves = []
    for d in range(Z * PLANE):
        z, y, x, c = d // PLANE, d // (X * C) % Y, d // C % X, d % C
        z, y, x, c = target(z, y, x, c)
        moves.append((d, ((z % Z * Y + y % Y) * X + x) * C + c))
    return moves


def dot(a, b, dims):
    return lax.dot_general(a, b, dims, preferred_element_type=jnp.float32)


def pack(block):
    half = block.shape[0] // 2
    return jnp.concatenate([block[:half], block[half:]], axis=1)


def unpack(block):
    half = block.shape[1] // 2
    return [block, jnp.concatenate([block[:, half:], block[:, :half]], axis=1)]


def load(copies, sems):
    pending = [
        pltpu.make_async_copy(source, target, sems.at[i]) for i, (source, target) in enumerate(copies)
    ]
    for copy in pending:
        copy.start()
    return pending


SMEM_SPEC = pl.BlockSpec(memory_space=pltpu.SMEM)
VMEM_SPEC = pl.BlockSpec(memory_space=pltpu.VMEM)
ANY_SPEC = pl.BlockSpec(memory_space=pl.ANY)


def cost(flops, moved):
    return pl.CostEstimate(flops=flops, bytes_accessed=moved, transcendentals=0)


def tables_kernel(lists, wanted_out):
    own = lax.axis_index("loop") % PLANE
    count = 2 * lists.shape[2]
    devices = jnp.concatenate([lists[0], lists[1]], axis=1)
    members = jnp.concatenate([lists[2], lists[3]], axis=1)
    flat = lax.broadcasted_iota(jnp.int32, devices.shape, 1)
    lane = lax.broadcasted_iota(jnp.int32, wanted_out.shape, 1)
    table = jnp.zeros(wanted_out.shape, jnp.int32)
    for z in range(Z):
        place = jnp.where(devices == z * PLANE + own, flat, count)
        lowest = jnp.min(place, axis=1, keepdims=True)
        place_two = jnp.where(place > lowest, place, count)
        second = jnp.min(place_two, axis=1, keepdims=True)
        for k, at in enumerate((lowest, second)):
            member = jnp.sum(jnp.where(flat == at, members, 0), axis=1, keepdims=True)
            table = jnp.where(lane == z * 2 + k, member, table)
    wanted_out[...] = table


def tables(lists):
    return pl.pallas_call(
        tables_kernel,
        out_shape=jax.ShapeDtypeStruct((PLANE, 128), jnp.int32),
        in_specs=[VMEM_SPEC],
        out_specs=VMEM_SPEC,
        compiler_params=pltpu.CompilerParams(vmem_limit_bytes=8 * MIB),
        cost_estimate=cost(2_000_000, 20_000),
        name="tables",
    )(lists)


def upward_kernel(
    parent, own_list, peer_list, signals_in, basis_in, transfer_in, coef_out, pay_out, row_out, signals, basis, transfer, packed, sems, out_sems
):
    pending = load([(signals_in, signals), (basis_in, basis), (transfer_in, transfer)], sems)
    lists = []
    for ref in (own_list, peer_list):
        ids = ref[...]
        row = jnp.concatenate([ids[t : t + 1] for t in range(ids.shape[0])], axis=1)
        row = jnp.concatenate([row, jnp.full((1, 256 - row.shape[1]), -8, jnp.int32)], axis=1)
        devices, members = row // ids.shape[0], row % ids.shape[0]
        lists += [devices[:, :128], devices[:, 128:], members[:, :128], members[:, 128:]]
        if ref is own_list:
            row_out[...] = devices
    lists.append(jnp.zeros((8, 128), jnp.int32))
    pay_out[64:80] = jnp.concatenate(lists, axis=0).astype(jnp.float32).astype(jnp.bfloat16)
    for copy in pending:
        copy.wait()
    leaf_count, rank, leaf_size = basis.shape
    coefs = []
    for c in range(leaf_count):
        block = signals[:, c * leaf_size : (c + 1) * leaf_size]
        coefs.append(dot(basis[c], block, NT).astype(jnp.bfloat16))
    for c in range(leaf_count):
        packed[c] = pack(coefs[c])
    written = load([(packed, coef_out.at[z]) for z in range(Z)], out_sems)
    lifted = [dot(transfer[c], coefs[c], TN) for c in range(leaf_count)]
    sums = [jnp.zeros((rank, signals.shape[0]), jnp.float32) for _ in range(2)]
    for c in range(leaf_count):
        member = parent[c] - lax.axis_index("loop") * 2
        sums = [s + jnp.where(member == i, lifted[c], 0.0) for i, s in enumerate(sums)]
    for i, s in enumerate(sums):
        pay_out[i * 32 : (i + 1) * 32] = pack(s.astype(jnp.bfloat16))
    for copy in written:
        copy.wait()


def upward(parent, own_list, peer_list, signals, basis, transfer):
    leaf_count = basis.shape[0]
    return pl.pallas_call(
        upward_kernel,
        out_shape=(
            jax.ShapeDtypeStruct((Z, leaf_count, 32, 128), jnp.bfloat16),
            jax.ShapeDtypeStruct((80, 128), jnp.bfloat16),
            jax.ShapeDtypeStruct((1, 256), jnp.int32),
        ),
        in_specs=[SMEM_SPEC, VMEM_SPEC, VMEM_SPEC, ANY_SPEC, ANY_SPEC, ANY_SPEC],
        out_specs=(ANY_SPEC, VMEM_SPEC, VMEM_SPEC),
        scratch_shapes=[
            pltpu.VMEM(signals.shape, jnp.bfloat16),
            pltpu.VMEM(basis.shape, jnp.bfloat16),
            pltpu.VMEM(transfer.shape, jnp.bfloat16),
            pltpu.VMEM((leaf_count, 32, 128), jnp.bfloat16),
            pltpu.SemaphoreType.DMA((3,)),
            pltpu.SemaphoreType.DMA((Z,)),
        ],
        compiler_params=pltpu.CompilerParams(vmem_limit_bytes=56 * MIB),
        cost_estimate=cost(30_000_000, 700_000),
        name="upward",
    )(parent, own_list, peer_list, signals, basis, transfer)


def select_kernel(wanted, planes, send_out, send, sems):
    own = lax.axis_index("loop") % PLANE
    pending = []
    for peer in range(PLANE):
        dy = jnp.bitwise_and(peer // (X * C) - own // (X * C) + Y, Y - 1)
        row = dy * (X * C) + jnp.bitwise_and(jnp.bitwise_xor(peer, own), X * C - 1)
        for slot in range(2 * Z):
            send[peer, slot] = planes[slot // 2, wanted[row, slot]]
        pending.append(pltpu.make_async_copy(send.at[peer], send_out.at[peer], sems.at[peer]))
        pending[-1].start()
    for copy in pending:
        copy.wait()


def select(wanted, planes):
    shape = (PLANE, 2 * Z, 32, 128)
    return pl.pallas_call(
        select_kernel,
        out_shape=jax.ShapeDtypeStruct(shape, jnp.bfloat16),
        in_specs=[SMEM_SPEC, VMEM_SPEC],
        out_specs=ANY_SPEC,
        scratch_shapes=[pltpu.VMEM(shape, jnp.bfloat16), pltpu.SemaphoreType.DMA((PLANE,))],
        compiler_params=pltpu.CompilerParams(vmem_limit_bytes=8 * MIB),
        cost_estimate=cost(1_000_000, 2_500_000),
        name="select",
    )(wanted, planes)


def near_kernel(
    near_list, own_row, signals, other, before, after, tiles, own_out, other_out, slot_out, extended, sems
):
    half, width = signals.shape
    reach = before.shape[1]
    leaf_count, near_count, leaf_size, _ = tiles.shape
    pending = load(
        [
            (before, extended.at[:, :reach]),
            (signals, extended.at[:half, reach : reach + width]),
            (other, extended.at[half:, reach : reach + width]),
            (after, extended.at[:, reach + width :]),
        ],
        sems,
    )
    for copy in pending:
        copy.wait()
    row = own_row[...]
    size = row.shape[1]
    at_col = lax.broadcasted_iota(jnp.int32, (size, size), 0)
    at_row = lax.broadcasted_iota(jnp.int32, (size, size), 1)
    column = jnp.sum(jnp.where(at_col == at_row, row, 0), axis=1, keepdims=True)
    earlier = jnp.where((column == row) & (at_col < at_row), 1, 0)
    seen = jnp.sum(earlier, axis=0, keepdims=True)
    slot_out[...] = row % PLANE * (2 * Z) + row // PLANE * 2 + seen
    loop, rhs = lax.axis_index("loop"), lax.axis_index("rhs")
    leaves = leaf_count * Z * PLANE
    for t in range(leaf_count):
        total = jnp.zeros((2 * half, leaf_size), jnp.float32)
        for j in range(near_count):
            source = near_list[t, rhs * near_count + j]
            at = (source - loop * leaf_count + leaf_count // 2 + leaves) % leaves
            block = extended[:, pl.ds(pl.multiple_of(at * leaf_size, leaf_size), leaf_size)]
            total = total + dot(block, tiles[t, j], NT)
        own_out[:, t * leaf_size : (t + 1) * leaf_size] = total[:half]
        other_out[:, t * leaf_size : (t + 1) * leaf_size] = total[half:].astype(jnp.bfloat16)


def near_field(near_list, own_row, signals, other, before, after, tiles):
    half, width = signals.shape
    return pl.pallas_call(
        near_kernel,
        out_shape=(
            jax.ShapeDtypeStruct((half, width), jnp.float32),
            jax.ShapeDtypeStruct((half, width), jnp.bfloat16),
            jax.ShapeDtypeStruct(own_row.shape, jnp.int32),
        ),
        in_specs=[SMEM_SPEC, VMEM_SPEC, ANY_SPEC, ANY_SPEC, ANY_SPEC, ANY_SPEC, VMEM_SPEC],
        out_specs=(VMEM_SPEC,) * 3,
        scratch_shapes=[
            pltpu.VMEM((2 * half, 2 * width), jnp.bfloat16),
            pltpu.SemaphoreType.DMA((4,)),
        ],
        compiler_params=pltpu.CompilerParams(vmem_limit_bytes=12 * MIB),
        cost_estimate=cost(600_000_000, 10_000_000),
        name="near_field",
    )(near_list, own_row, signals, other, before, after, tiles)


def fields_kernel(parent, parent_far, *refs):
    sources = refs[:10]
    coupling, transfer, out, parents = refs[10:]
    at = 0
    for ref in sources:
        parents[at : at + ref.shape[0]] = ref[...]
        at += ref.shape[0]
    me = lax.axis_index("loop")
    own_plane = me % PLANE
    per = 2 * Y * X
    columns = out.shape[2]
    results = []
    for p in range(parent_far.shape[0]):
        stacked = []
        for j in range(parent_far.shape[1]):
            source = parent_far[p, j]
            device = source // 2
            hop = jnp.bitwise_and(device // PLANE - me // PLANE + Z, Z - 1)
            dy = jnp.bitwise_and(device // (X * C) - own_plane // (X * C) + Y, Y - 1)
            cross = jnp.bitwise_xor(device, own_plane)
            dx = jnp.bitwise_and(cross // C, X - 1)
            member = (dy * X + dx) * 2 + jnp.bitwise_and(source, 1)
            base = jnp.int32(0)
            for place, h in enumerate((0, 1, 7, 2, 6, 3, 5, 4)):
                base = jnp.where(hop == h, place * per, base)
            where = jnp.bitwise_and(cross, C - 1) * (Z * per) + base + member
            stacked += unpack(parents[where])
        field = dot(coupling[p], jnp.concatenate(stacked, axis=0), NN)
        results.append(field[:, :columns].astype(jnp.bfloat16))
    for c in range(transfer.shape[0]):
        field = jnp.where(parent[c] == me * 2, results[0], results[1])
        out[c] = dot(transfer[c], field, NN)


def fields(parent, parent_far, pieces, parent_coupling, transfer):
    return pl.pallas_call(
        fields_kernel,
        out_shape=jax.ShapeDtypeStruct(transfer.shape, jnp.float32),
        in_specs=[SMEM_SPEC] * 2 + [VMEM_SPEC] * 12,
        out_specs=VMEM_SPEC,
        scratch_shapes=[pltpu.VMEM((2 * Z * Y * X * 2, 32, 128), jnp.bfloat16)],
        compiler_params=pltpu.CompilerParams(vmem_limit_bytes=16 * MIB),
        cost_estimate=cost(50_000_000, 4_000_000),
        name="fields",
    )(parent, parent_far, *pieces, parent_coupling, transfer)


def downward_kernel(
    slots,
    blocks_in,
    coupling_in,
    descended_in,
    basis_in,
    near_own_in,
    out_hbm,
    blocks,
    coupling,
    descended,
    basis,
    near_own,
    stacked,
    out,
    sems,
    out_sems,
):
    leaf_count, rank, leaf_size = basis.shape
    part = blocks.shape[0] // 8
    pending = load(
        [(blocks_in.at[pl.ds(i * part, part)], blocks.at[pl.ds(i * part, part)]) for i in range(8)]
        + [(coupling_in.at[c], coupling.at[c]) for c in range(leaf_count)]
        + [(descended_in, descended), (basis_in, basis), (near_own_in, near_own)],
        sems,
    )
    for copy in pending[:8]:
        copy.wait()
    sources = coupling.shape[2] // rank
    columns = out.shape[0]
    for c in range(leaf_count):
        for j in range(sources):
            pieces = jnp.concatenate(unpack(blocks[slots[0, c * sources + j]]), axis=0)
            stacked[c, j * rank : (j + 1) * rank] = pieces
    for copy in pending[8:]:
        copy.wait()
    far = [dot(coupling[c], stacked[c], NN)[:, :columns] for c in range(leaf_count)]
    combined = [(far[c] + descended[c]).astype(jnp.bfloat16) for c in range(leaf_count)]
    written = []
    for c in range(leaf_count):
        at = pl.ds(c * leaf_size, leaf_size)
        out[:, at] = near_own[:, at] + dot(combined[c], basis[c], TN)
        written.append(pltpu.make_async_copy(out.at[:, at], out_hbm.at[:, at], out_sems.at[c]))
        written[-1].start()
    for copy in written:
        copy.wait()


def downward(slots, blocks, coupling, descended, basis, near_own):
    arrays = (blocks, coupling, descended, basis, near_own)
    leaf_count = basis.shape[0]
    return pl.pallas_call(
        downward_kernel,
        out_shape=jax.ShapeDtypeStruct(near_own.shape, jnp.float32),
        in_specs=[SMEM_SPEC] + [ANY_SPEC] * 5,
        out_specs=ANY_SPEC,
        scratch_shapes=[pltpu.VMEM(a.shape, a.dtype) for a in arrays]
        + [
            pltpu.VMEM((leaf_count, coupling.shape[2], 128), jnp.bfloat16),
            pltpu.VMEM(near_own.shape, jnp.float32),
            pltpu.SemaphoreType.DMA((11 + leaf_count,)),
            pltpu.SemaphoreType.DMA((leaf_count,)),
        ],
        compiler_params=pltpu.CompilerParams(vmem_limit_bytes=62 * MIB),
        cost_estimate=cost(150_000_000, 6_000_000),
        name="downward",
    )(slots, *arrays)


def shards(
    signals,
    near_tiles,
    near_list,
    leaf_basis,
    transfer,
    parent,
    coupling,
    far_list,
    parent_coupling,
    parent_far,
):
    width = signals.shape[1]
    leaf_count = leaf_basis.shape[0]
    along = functools.partial(lax.ppermute, axis_name="loop")
    swap = functools.partial(lax.ppermute, axis_name="rhs", perm=[(0, 1), (1, 0)])
    x_swap = loop_moves(lambda z, y, x, c: (z, y, 1 - x, c))
    c_swap = loop_moves(lambda z, y, x, c: (z, y, x, 1 - c))
    columns_of = [[z * PLANE + p for z in range(Z)] for p in range(PLANE)]
    planes_of = [[z * PLANE + p for p in range(PLANE)] for z in range(Z)]

    other = swap(signals)
    peer_list = along(far_list, perm=c_swap)
    coefs, payload, own_row = upward(parent, far_list, peer_list, signals, leaf_basis, transfer)

    planes = lax.all_to_all(coefs, "loop", 0, 0, tiled=True, axis_index_groups=columns_of)
    pair = jnp.stack([payload, along(payload, perm=x_swap)])
    quads = jnp.stack(
        [pair]
        + [
            along(pair, perm=loop_moves(lambda z, y, x, c, dy=dy: (z, y - dy, x, c)))
            for dy in range(1, Y)
        ]
    )
    plane_lists = quads[:, :, 64:72].reshape(PLANE, 4, 128).transpose(1, 0, 2)
    parents = quads[:, :, :64].reshape(-1, 32, 128)
    down = functools.partial(along, perm=loop_moves(lambda z, y, x, c: (z - 1, y, x, c)))
    up = functools.partial(along, perm=loop_moves(lambda z, y, x, c: (z + 1, y, x, c)))
    one_down, one_up = down(parents), up(parents)

    reach = width // 2
    count = Z * PLANE
    before = along(
        jnp.concatenate([signals[:, reach:], other[:, reach:]]), perm=[(i, (i + 1) % count) for i in range(count)]
    )
    after = along(
        jnp.concatenate([signals[:, :reach], other[:, :reach]]), perm=[((i + 1) % count, i) for i in range(count)]
    )
    wanted = tables(plane_lists.astype(jnp.int32))
    send = select(wanted, planes)
    _, one_down, one_up, before, after = lax.optimization_barrier((send, one_down, one_up, before, after))
    blocks = lax.all_to_all(send, "loop", 0, 0, tiled=True, axis_index_groups=planes_of)

    two_down, two_up = down(one_down), up(one_up)
    near_own, near_other, slots = near_field(near_list, own_row, signals, other, before, after, near_tiles)
    near_in = swap(near_other)
    _, two_down, two_up = lax.optimization_barrier((near_other, two_down, two_up))
    three_down, three_up = down(two_down), up(two_up)
    half = parents.shape[0] // 2
    four_down = along(two_down[:half], perm=loop_moves(lambda z, y, x, c: (z - 2, y, x, c)))
    four_up = along(two_up[half:], perm=loop_moves(lambda z, y, x, c: (z + 2, y, x, c)))
    mine = [parents, one_down, one_up, two_down, two_up, three_down, three_up, four_down, four_up]
    theirs = [along(jnp.concatenate(mine), perm=c_swap)]
    descended = fields(parent, parent_far, mine + theirs, parent_coupling, transfer)

    partial = downward(slots, blocks.reshape(-1, 32, 128), coupling, descended, leaf_basis, near_own)
    return (partial + near_in.astype(jnp.float32)).astype(jnp.bfloat16)


def solution(mesh):
    in_specs = (
        P("rhs", "loop"),
        P("loop", "rhs", None, None),
        P("loop", None),
        P("loop", None, None),
        P("loop", None, None),
        P("loop"),
        P("loop", None, None),
        P("loop", None),
        P("loop", None, None),
        P("loop", None),
    )
    out_specs = P("rhs", "loop")
    return jax.shard_map(shards, mesh=mesh, in_specs=in_specs, out_specs=out_specs, check_vma=False)
```

```python
import functools

import jax
import jax.numpy as jnp
from jax import lax
from jax.experimental import pallas as pl
from jax.experimental.pallas import tpu as pltpu
from jax.sharding import PartitionSpec as P

Z, Y, X, C = 8, 4, 2, 2
PLANE = Y * X * C
MIB = 1 << 20
NT = (((1,), (1,)), ((), ()))
TN = (((0,), (0,)), ((), ()))
NN = (((1,), (0,)), ((), ()))


def loop_moves(target):
    moves = []
    for d in range(Z * PLANE):
        z, y, x, c = d // PLANE, d // (X * C) % Y, d // C % X, d % C
        z, y, x, c = target(z, y, x, c)
        moves.append((d, ((z % Z * Y + y % Y) * X + x) * C + c))
    return moves


def dot(a, b, dims):
    return lax.dot_general(a, b, dims, preferred_element_type=jnp.float32)


def pack(block):
    half = block.shape[0] // 2
    return jnp.concatenate([block[:half], block[half:]], axis=1)


def unpack(block):
    half = block.shape[1] // 2
    return [block, jnp.concatenate([block[:, half:], block[:, :half]], axis=1)]


def load(copies, sems):
    pending = [
        pltpu.make_async_copy(source, target, sems.at[i]) for i, (source, target) in enumerate(copies)
    ]
    for copy in pending:
        copy.start()
    return pending


SMEM_SPEC = pl.BlockSpec(memory_space=pltpu.SMEM)
VMEM_SPEC = pl.BlockSpec(memory_space=pltpu.VMEM)
ANY_SPEC = pl.BlockSpec(memory_space=pl.ANY)


def cost(flops, moved):
    return pl.CostEstimate(flops=flops, bytes_accessed=moved, transcendentals=0)


def tables_kernel(lists, wanted_out):
    own = lax.axis_index("loop") % PLANE
    count = 2 * lists.shape[2]
    devices = jnp.concatenate([lists[0], lists[1]], axis=1)
    members = jnp.concatenate([lists[2], lists[3]], axis=1)
    flat = lax.broadcasted_iota(jnp.int32, devices.shape, 1)
    lane = lax.broadcasted_iota(jnp.int32, wanted_out.shape, 1)
    table = jnp.zeros(wanted_out.shape, jnp.int32)
    for z in range(Z):
        place = jnp.where(devices == z * PLANE + own, flat, count)
        lowest = jnp.min(place, axis=1, keepdims=True)
        place_two = jnp.where(place > lowest, place, count)
        second = jnp.min(place_two, axis=1, keepdims=True)
        for k, at in enumerate((lowest, second)):
            member = jnp.sum(jnp.where(flat == at, members, 0), axis=1, keepdims=True)
            table = jnp.where(lane == z * 2 + k, member, table)
    wanted_out[...] = table


def tables(lists):
    return pl.pallas_call(
        tables_kernel,
        out_shape=jax.ShapeDtypeStruct((PLANE, 128), jnp.int32),
        in_specs=[VMEM_SPEC],
        out_specs=VMEM_SPEC,
        compiler_params=pltpu.CompilerParams(vmem_limit_bytes=8 * MIB),
        cost_estimate=cost(2_000_000, 20_000),
        name="tables",
    )(lists)


def upward_kernel(
    parent_in,
    own_list_in,
    peer_list_in,
    signals_in,
    basis_in,
    transfer_in,
    coef_out,
    pay_out,
    row_out,
    parent,
    own_list,
    peer_list,
    signals,
    basis,
    transfer,
    packed,
    pay,
    row_held,
    sems,
    out_sems,
):
    pending = load(
        [
            (signals_in, signals),
            (basis_in, basis),
            (own_list_in, own_list),
            (peer_list_in, peer_list),
            (transfer_in, transfer),
            (parent_in, parent),
        ],
        sems,
    )
    pending[2].wait()
    pending[3].wait()
    lists = []
    for ref in (own_list, peer_list):
        ids = ref[...]
        row = jnp.concatenate([ids[t : t + 1] for t in range(ids.shape[0])], axis=1)
        row = jnp.concatenate([row, jnp.full((1, 256 - row.shape[1]), -8, jnp.int32)], axis=1)
        devices, members = row // ids.shape[0], row % ids.shape[0]
        lists += [devices[:, :128], devices[:, 128:], members[:, :128], members[:, 128:]]
        if ref is own_list:
            row_held[...] = devices
    lists.append(jnp.zeros((8, 128), jnp.int32))
    pay[64:80] = jnp.concatenate(lists, axis=0).astype(jnp.float32).astype(jnp.bfloat16)
    written = load([(row_held, row_out)], out_sems)
    pending[0].wait()
    pending[1].wait()
    leaf_count, rank, leaf_size = basis.shape
    coefs = []
    for c in range(leaf_count):
        block = signals[:, c * leaf_size : (c + 1) * leaf_size]
        coefs.append(dot(basis[c], block, NT).astype(jnp.bfloat16))
    for c in range(leaf_count):
        packed[c] = pack(coefs[c])
    written += load([(packed, coef_out.at[z]) for z in range(Z)], out_sems.at[pl.ds(1, Z)])
    pending[4].wait()
    pending[5].wait()
    lifted = [dot(transfer[c], coefs[c], TN) for c in range(leaf_count)]
    sums = [jnp.zeros((rank, signals.shape[0]), jnp.float32) for _ in range(2)]
    for c in range(leaf_count):
        member = parent[c] - lax.axis_index("loop") * 2
        sums = [s + jnp.where(member == i, lifted[c], 0.0) for i, s in enumerate(sums)]
    for i, s in enumerate(sums):
        pay[i * 32 : (i + 1) * 32] = pack(s.astype(jnp.bfloat16))
    written += load([(pay, pay_out)], out_sems.at[pl.ds(1 + Z, 1)])
    for copy in written:
        copy.wait()


def upward(parent, own_list, peer_list, signals, basis, transfer):
    leaf_count = basis.shape[0]
    return pl.pallas_call(
        upward_kernel,
        out_shape=(
            jax.ShapeDtypeStruct((Z, leaf_count, 32, 128), jnp.bfloat16),
            jax.ShapeDtypeStruct((80, 128), jnp.bfloat16),
            jax.ShapeDtypeStruct((1, 256), jnp.int32),
        ),
        in_specs=[ANY_SPEC] * 6,
        out_specs=(ANY_SPEC,) * 3,
        scratch_shapes=[
            pltpu.SMEM(parent.shape, jnp.int32),
            pltpu.VMEM(own_list.shape, jnp.int32),
            pltpu.VMEM(own_list.shape, jnp.int32),
            pltpu.VMEM(signals.shape, jnp.bfloat16),
            pltpu.VMEM(basis.shape, jnp.bfloat16),
            pltpu.VMEM(transfer.shape, jnp.bfloat16),
            pltpu.VMEM((leaf_count, 32, 128), jnp.bfloat16),
            pltpu.VMEM((80, 128), jnp.bfloat16),
            pltpu.VMEM((1, 256), jnp.int32),
            pltpu.SemaphoreType.DMA((6,)),
            pltpu.SemaphoreType.DMA((2 + Z,)),
        ],
        compiler_params=pltpu.CompilerParams(vmem_limit_bytes=56 * MIB),
        cost_estimate=cost(30_000_000, 700_000),
        name="upward",
    )(parent, own_list, peer_list, signals, basis, transfer)


def select_kernel(wanted, planes, send_out, send, sems):
    own = lax.axis_index("loop") % PLANE
    pending = []
    for peer in range(PLANE):
        dy = jnp.bitwise_and(peer // (X * C) - own // (X * C) + Y, Y - 1)
        row = dy * (X * C) + jnp.bitwise_and(jnp.bitwise_xor(peer, own), X * C - 1)
        for slot in range(2 * Z):
            send[peer, slot] = planes[slot // 2, wanted[row, slot]]
        pending.append(pltpu.make_async_copy(send.at[peer], send_out.at[peer], sems.at[peer]))
        pending[-1].start()
    for copy in pending:
        copy.wait()


def select(wanted, planes):
    shape = (PLANE, 2 * Z, 32, 128)
    return pl.pallas_call(
        select_kernel,
        out_shape=jax.ShapeDtypeStruct(shape, jnp.bfloat16),
        in_specs=[SMEM_SPEC, VMEM_SPEC],
        out_specs=ANY_SPEC,
        scratch_shapes=[pltpu.VMEM(shape, jnp.bfloat16), pltpu.SemaphoreType.DMA((PLANE,))],
        compiler_params=pltpu.CompilerParams(vmem_limit_bytes=8 * MIB),
        cost_estimate=cost(1_000_000, 2_500_000),
        name="select",
    )(wanted, planes)


def near_kernel(
    near_list, own_row, signals, other, before, after, tiles, own_out, other_out, slot_out, extended, sems
):
    half, width = signals.shape
    reach = before.shape[1]
    leaf_count, near_count, leaf_size, _ = tiles.shape
    pending = load(
        [
            (before, extended.at[:, :reach]),
            (signals, extended.at[:half, reach : reach + width]),
            (other, extended.at[half:, reach : reach + width]),
            (after, extended.at[:, reach + width :]),
        ],
        sems,
    )
    for copy in pending:
        copy.wait()
    row = own_row[...]
    size = row.shape[1]
    at_col = lax.broadcasted_iota(jnp.int32, (size, size), 0)
    at_row = lax.broadcasted_iota(jnp.int32, (size, size), 1)
    column = jnp.sum(jnp.where(at_col == at_row, row, 0), axis=1, keepdims=True)
    earlier = jnp.where((column == row) & (at_col < at_row), 1, 0)
    seen = jnp.sum(earlier, axis=0, keepdims=True)
    slot_out[...] = row % PLANE * (2 * Z) + row // PLANE * 2 + seen
    loop, rhs = lax.axis_index("loop"), lax.axis_index("rhs")
    leaves = leaf_count * Z * PLANE
    for t in range(leaf_count):
        total = jnp.zeros((2 * half, leaf_size), jnp.float32)
        for j in range(near_count):
            source = near_list[t, rhs * near_count + j]
            at = (source - loop * leaf_count + leaf_count // 2 + leaves) % leaves
            block = extended[:, pl.ds(pl.multiple_of(at * leaf_size, leaf_size), leaf_size)]
            total = total + dot(block, tiles[t, j], NT)
        own_out[:, t * leaf_size : (t + 1) * leaf_size] = total[:half]
        other_out[:, t * leaf_size : (t + 1) * leaf_size] = total[half:].astype(jnp.bfloat16)


def near_field(near_list, own_row, signals, other, before, after, tiles):
    half, width = signals.shape
    return pl.pallas_call(
        near_kernel,
        out_shape=(
            jax.ShapeDtypeStruct((half, width), jnp.float32),
            jax.ShapeDtypeStruct((half, width), jnp.bfloat16),
            jax.ShapeDtypeStruct(own_row.shape, jnp.int32),
        ),
        in_specs=[SMEM_SPEC, VMEM_SPEC, ANY_SPEC, ANY_SPEC, ANY_SPEC, ANY_SPEC, VMEM_SPEC],
        out_specs=(VMEM_SPEC,) * 3,
        scratch_shapes=[
            pltpu.VMEM((2 * half, 2 * width), jnp.bfloat16),
            pltpu.SemaphoreType.DMA((4,)),
        ],
        compiler_params=pltpu.CompilerParams(vmem_limit_bytes=12 * MIB),
        cost_estimate=cost(600_000_000, 10_000_000),
        name="near_field",
    )(near_list, own_row, signals, other, before, after, tiles)


def fields_kernel(parent, parent_far, *refs):
    sources = refs[:10]
    coupling, transfer, out, parents = refs[10:]
    at = 0
    for ref in sources:
        parents[at : at + ref.shape[0]] = ref[...]
        at += ref.shape[0]
    me = lax.axis_index("loop")
    own_plane = me % PLANE
    per = 2 * Y * X
    columns = out.shape[2]
    results = []
    for p in range(parent_far.shape[0]):
        stacked = []
        for j in range(parent_far.shape[1]):
            source = parent_far[p, j]
            device = source // 2
            hop = jnp.bitwise_and(device // PLANE - me // PLANE + Z, Z - 1)
            dy = jnp.bitwise_and(device // (X * C) - own_plane // (X * C) + Y, Y - 1)
            cross = jnp.bitwise_xor(device, own_plane)
            dx = jnp.bitwise_and(cross // C, X - 1)
            member = (dy * X + dx) * 2 + jnp.bitwise_and(source, 1)
            base = jnp.int32(0)
            for place, h in enumerate((0, 1, 7, 2, 6, 3, 5, 4)):
                base = jnp.where(hop == h, place * per, base)
            where = jnp.bitwise_and(cross, C - 1) * (Z * per) + base + member
            stacked += unpack(parents[where])
        field = dot(coupling[p], jnp.concatenate(stacked, axis=0), NN)
        results.append(field[:, :columns].astype(jnp.bfloat16))
    for c in range(transfer.shape[0]):
        field = jnp.where(parent[c] == me * 2, results[0], results[1])
        out[c] = dot(transfer[c], field, NN)


def fields(parent, parent_far, pieces, parent_coupling, transfer):
    return pl.pallas_call(
        fields_kernel,
        out_shape=jax.ShapeDtypeStruct(transfer.shape, jnp.float32),
        in_specs=[SMEM_SPEC] * 2 + [VMEM_SPEC] * 12,
        out_specs=VMEM_SPEC,
        scratch_shapes=[pltpu.VMEM((2 * Z * Y * X * 2, 32, 128), jnp.bfloat16)],
        compiler_params=pltpu.CompilerParams(vmem_limit_bytes=16 * MIB),
        cost_estimate=cost(50_000_000, 4_000_000),
        name="fields",
    )(parent, parent_far, *pieces, parent_coupling, transfer)


def downward_kernel(
    slots_in,
    blocks_in,
    coupling_in,
    descended_in,
    basis_in,
    near_own_in,
    out_hbm,
    slots,
    blocks,
    coupling,
    descended,
    basis,
    near_own,
    stacked,
    out,
    sems,
    out_sems,
):
    leaf_count, rank, leaf_size = basis.shape
    part = blocks.shape[0] // 8
    pending = load(
        [(blocks_in.at[pl.ds(i * part, part)], blocks.at[pl.ds(i * part, part)]) for i in range(8)]
        + [(coupling_in.at[c], coupling.at[c]) for c in range(leaf_count)]
        + [(descended_in, descended), (basis_in, basis), (near_own_in, near_own), (slots_in, slots)],
        sems,
    )
    for copy in pending[:8] + pending[-1:]:
        copy.wait()
    sources = coupling.shape[2] // rank
    columns = out.shape[0]
    for c in range(leaf_count):
        for j in range(sources):
            pieces = jnp.concatenate(unpack(blocks[slots[0, c * sources + j]]), axis=0)
            stacked[c, j * rank : (j + 1) * rank] = pieces
    for copy in pending[8:-1]:
        copy.wait()
    far = [dot(coupling[c], stacked[c], NN)[:, :columns] for c in range(leaf_count)]
    combined = [(far[c] + descended[c]).astype(jnp.bfloat16) for c in range(leaf_count)]
    written = []
    for c in range(leaf_count):
        at = pl.ds(c * leaf_size, leaf_size)
        out[:, at] = near_own[:, at] + dot(combined[c], basis[c], TN)
        written.append(pltpu.make_async_copy(out.at[:, at], out_hbm.at[:, at], out_sems.at[c]))
        written[-1].start()
    for copy in written:
        copy.wait()


def downward(slots, blocks, coupling, descended, basis, near_own):
    arrays = (blocks, coupling, descended, basis, near_own)
    leaf_count = basis.shape[0]
    return pl.pallas_call(
        downward_kernel,
        out_shape=jax.ShapeDtypeStruct(near_own.shape, jnp.float32),
        in_specs=[ANY_SPEC] * 6,
        out_specs=ANY_SPEC,
        scratch_shapes=[pltpu.SMEM(slots.shape, jnp.int32)]
        + [pltpu.VMEM(a.shape, a.dtype) for a in arrays]
        + [
            pltpu.VMEM((leaf_count, coupling.shape[2], 128), jnp.bfloat16),
            pltpu.VMEM(near_own.shape, jnp.float32),
            pltpu.SemaphoreType.DMA((12 + leaf_count,)),
            pltpu.SemaphoreType.DMA((leaf_count,)),
        ],
        compiler_params=pltpu.CompilerParams(vmem_limit_bytes=62 * MIB),
        cost_estimate=cost(150_000_000, 6_000_000),
        name="downward",
    )(slots, *arrays)


def shards(
    signals,
    near_tiles,
    near_list,
    leaf_basis,
    transfer,
    parent,
    coupling,
    far_list,
    parent_coupling,
    parent_far,
):
    width = signals.shape[1]
    leaf_count = leaf_basis.shape[0]
    along = functools.partial(lax.ppermute, axis_name="loop")
    swap = functools.partial(lax.ppermute, axis_name="rhs", perm=[(0, 1), (1, 0)])
    x_swap = loop_moves(lambda z, y, x, c: (z, y, 1 - x, c))
    c_swap = loop_moves(lambda z, y, x, c: (z, y, x, 1 - c))
    columns_of = [[z * PLANE + p for z in range(Z)] for p in range(PLANE)]
    planes_of = [[z * PLANE + p for p in range(PLANE)] for z in range(Z)]

    other = swap(signals)
    peer_list = along(far_list, perm=c_swap)
    coefs, payload, own_row = upward(parent, far_list, peer_list, signals, leaf_basis, transfer)

    planes = lax.all_to_all(coefs, "loop", 0, 0, tiled=True, axis_index_groups=columns_of)
    pair = jnp.stack([payload, along(payload, perm=x_swap)])
    quads = jnp.stack(
        [pair]
        + [
            along(pair, perm=loop_moves(lambda z, y, x, c, dy=dy: (z, y - dy, x, c)))
            for dy in range(1, Y)
        ]
    )
    plane_lists = quads[:, :, 64:72].reshape(PLANE, 4, 128).transpose(1, 0, 2)
    parents = quads[:, :, :64].reshape(-1, 32, 128)
    down = functools.partial(along, perm=loop_moves(lambda z, y, x, c: (z - 1, y, x, c)))
    up = functools.partial(along, perm=loop_moves(lambda z, y, x, c: (z + 1, y, x, c)))
    one_down, one_up = down(parents), up(parents)

    reach = width // 2
    count = Z * PLANE
    before = along(
        jnp.concatenate([signals[:, reach:], other[:, reach:]]), perm=[(i, (i + 1) % count) for i in range(count)]
    )
    after = along(
        jnp.concatenate([signals[:, :reach], other[:, :reach]]), perm=[((i + 1) % count, i) for i in range(count)]
    )
    wanted = tables(plane_lists.astype(jnp.int32))
    send = select(wanted, planes)
    _, one_down, one_up, before, after = lax.optimization_barrier((send, one_down, one_up, before, after))
    blocks = lax.all_to_all(send, "loop", 0, 0, tiled=True, axis_index_groups=planes_of)

    two_down, two_up = down(one_down), up(one_up)
    near_own, near_other, slots = near_field(near_list, own_row, signals, other, before, after, near_tiles)
    near_in = swap(near_other)
    _, two_down, two_up = lax.optimization_barrier((near_other, two_down, two_up))
    three_down, three_up = down(two_down), up(two_up)
    half = parents.shape[0] // 2
    four_down = along(two_down[:half], perm=loop_moves(lambda z, y, x, c: (z - 2, y, x, c)))
    four_up = along(two_up[half:], perm=loop_moves(lambda z, y, x, c: (z + 2, y, x, c)))
    mine = [parents, one_down, one_up, two_down, two_up, three_down, three_up, four_down, four_up]
    theirs = [along(jnp.concatenate(mine), perm=c_swap)]
    descended = fields(parent, parent_far, mine + theirs, parent_coupling, transfer)

    partial = downward(slots, blocks.reshape(-1, 32, 128), coupling, descended, leaf_basis, near_own)
    return (partial + near_in.astype(jnp.float32)).astype(jnp.bfloat16)


def solution(mesh):
    in_specs = (
        P("rhs", "loop"),
        P("loop", "rhs", None, None),
        P("loop", None),
        P("loop", None, None),
        P("loop", None, None),
        P("loop"),
        P("loop", None, None),
        P("loop", None),
        P("loop", None, None),
        P("loop", None),
    )
    out_specs = P("rhs", "loop")
    return jax.shard_map(shards, mesh=mesh, in_specs=in_specs, out_specs=out_specs, check_vma=False)
```

```python
import functools

import jax
import jax.numpy as jnp
from jax import lax
from jax.experimental import pallas as pl
from jax.experimental.pallas import tpu as pltpu
from jax.sharding import PartitionSpec as P

Z, Y, X, C = 8, 4, 2, 2
PLANE = Y * X * C
MIB = 1 << 20
NT = (((1,), (1,)), ((), ()))
TN = (((0,), (0,)), ((), ()))
NN = (((1,), (0,)), ((), ()))


def loop_moves(target):
    moves = []
    for d in range(Z * PLANE):
        z, y, x, c = d // PLANE, d // (X * C) % Y, d // C % X, d % C
        z, y, x, c = target(z, y, x, c)
        moves.append((d, ((z % Z * Y + y % Y) * X + x) * C + c))
    return moves


def dot(a, b, dims):
    return lax.dot_general(a, b, dims, preferred_element_type=jnp.float32)


def pack(block):
    half = block.shape[0] // 2
    return jnp.concatenate([block[:half], block[half:]], axis=1)


def unpack(block):
    half = block.shape[1] // 2
    return [block, jnp.concatenate([block[:, half:], block[:, :half]], axis=1)]


def load(copies, sems):
    pending = [
        pltpu.make_async_copy(source, target, sems.at[i]) for i, (source, target) in enumerate(copies)
    ]
    for copy in pending:
        copy.start()
    return pending


SMEM_SPEC = pl.BlockSpec(memory_space=pltpu.SMEM)
VMEM_SPEC = pl.BlockSpec(memory_space=pltpu.VMEM)
ANY_SPEC = pl.BlockSpec(memory_space=pl.ANY)


def cost(flops, moved):
    return pl.CostEstimate(flops=flops, bytes_accessed=moved, transcendentals=0)


def tables_kernel(lists, wanted_out):
    own = lax.axis_index("loop") % PLANE
    count = 2 * lists.shape[2]
    devices = jnp.concatenate([lists[0], lists[1]], axis=1)
    members = jnp.concatenate([lists[2], lists[3]], axis=1)
    flat = lax.broadcasted_iota(jnp.int32, devices.shape, 1)
    lane = lax.broadcasted_iota(jnp.int32, wanted_out.shape, 1)
    table = jnp.zeros(wanted_out.shape, jnp.int32)
    for z in range(Z):
        place = jnp.where(devices == z * PLANE + own, flat, count)
        lowest = jnp.min(place, axis=1, keepdims=True)
        place_two = jnp.where(place > lowest, place, count)
        second = jnp.min(place_two, axis=1, keepdims=True)
        for k, at in enumerate((lowest, second)):
            member = jnp.sum(jnp.where(flat == at, members, 0), axis=1, keepdims=True)
            table = jnp.where(lane == z * 2 + k, member, table)
    wanted_out[...] = table


def tables(lists):
    return pl.pallas_call(
        tables_kernel,
        out_shape=jax.ShapeDtypeStruct((PLANE, 128), jnp.int32),
        in_specs=[VMEM_SPEC],
        out_specs=VMEM_SPEC,
        compiler_params=pltpu.CompilerParams(vmem_limit_bytes=8 * MIB),
        cost_estimate=cost(2_000_000, 20_000),
        name="tables",
    )(lists)


def upward_kernel(
    parent_in,
    own_list_in,
    peer_list_in,
    signals_in,
    basis_in,
    transfer_in,
    coef_out,
    pay_out,
    row_out,
    parent,
    own_list,
    peer_list,
    signals,
    basis,
    transfer,
    packed,
    pay,
    row_held,
    sems,
    out_sems,
):
    pending = load(
        [
            (signals_in, signals),
            (basis_in, basis),
            (own_list_in, own_list),
            (peer_list_in, peer_list),
            (transfer_in, transfer),
            (parent_in, parent),
        ],
        sems,
    )
    pending[2].wait()
    pending[3].wait()
    lists = []
    for ref in (own_list, peer_list):
        ids = ref[...]
        row = jnp.concatenate([ids[t : t + 1] for t in range(ids.shape[0])], axis=1)
        row = jnp.concatenate([row, jnp.full((1, 256 - row.shape[1]), -8, jnp.int32)], axis=1)
        devices, members = row // ids.shape[0], row % ids.shape[0]
        lists += [devices[:, :128], devices[:, 128:], members[:, :128], members[:, 128:]]
        if ref is own_list:
            row_held[...] = devices
    lists.append(jnp.zeros((8, 128), jnp.int32))
    pay[64:80] = jnp.concatenate(lists, axis=0).astype(jnp.float32).astype(jnp.bfloat16)
    written = load([(row_held, row_out)], out_sems)
    pending[0].wait()
    pending[1].wait()
    leaf_count, rank, leaf_size = basis.shape
    coefs = []
    for c in range(leaf_count):
        block = signals[:, c * leaf_size : (c + 1) * leaf_size]
        coefs.append(dot(basis[c], block, NT).astype(jnp.bfloat16))
    for c in range(leaf_count):
        packed[c] = pack(coefs[c])
    written += load([(packed, coef_out.at[z]) for z in range(Z)], out_sems.at[pl.ds(1, Z)])
    pending[4].wait()
    pending[5].wait()
    lifted = [dot(transfer[c], coefs[c], TN) for c in range(leaf_count)]
    sums = [jnp.zeros((rank, signals.shape[0]), jnp.float32) for _ in range(2)]
    for c in range(leaf_count):
        member = parent[c] - lax.axis_index("loop") * 2
        sums = [s + jnp.where(member == i, lifted[c], 0.0) for i, s in enumerate(sums)]
    for i, s in enumerate(sums):
        pay[i * 32 : (i + 1) * 32] = pack(s.astype(jnp.bfloat16))
    written += load([(pay, pay_out)], out_sems.at[pl.ds(1 + Z, 1)])
    for copy in written:
        copy.wait()


def upward(parent, own_list, peer_list, signals, basis, transfer):
    leaf_count = basis.shape[0]
    return pl.pallas_call(
        upward_kernel,
        out_shape=(
            jax.ShapeDtypeStruct((Z, leaf_count, 32, 128), jnp.bfloat16),
            jax.ShapeDtypeStruct((80, 128), jnp.bfloat16),
            jax.ShapeDtypeStruct((1, 256), jnp.int32),
        ),
        in_specs=[ANY_SPEC] * 6,
        out_specs=(ANY_SPEC,) * 3,
        scratch_shapes=[
            pltpu.SMEM(parent.shape, jnp.int32),
            pltpu.VMEM(own_list.shape, jnp.int32),
            pltpu.VMEM(own_list.shape, jnp.int32),
            pltpu.VMEM(signals.shape, jnp.bfloat16),
            pltpu.VMEM(basis.shape, jnp.bfloat16),
            pltpu.VMEM(transfer.shape, jnp.bfloat16),
            pltpu.VMEM((leaf_count, 32, 128), jnp.bfloat16),
            pltpu.VMEM((80, 128), jnp.bfloat16),
            pltpu.VMEM((1, 256), jnp.int32),
            pltpu.SemaphoreType.DMA((6,)),
            pltpu.SemaphoreType.DMA((2 + Z,)),
        ],
        compiler_params=pltpu.CompilerParams(vmem_limit_bytes=56 * MIB),
        cost_estimate=cost(30_000_000, 700_000),
        name="upward",
    )(parent, own_list, peer_list, signals, basis, transfer)


def select_kernel(wanted, planes, send_out, send, sems):
    own = lax.axis_index("loop") % PLANE
    pending = []
    for peer in range(PLANE):
        dy = jnp.bitwise_and(peer // (X * C) - own // (X * C) + Y, Y - 1)
        row = dy * (X * C) + jnp.bitwise_and(jnp.bitwise_xor(peer, own), X * C - 1)
        for slot in range(2 * Z):
            send[peer, slot] = planes[slot // 2, wanted[row, slot]]
        pending.append(pltpu.make_async_copy(send.at[peer], send_out.at[peer], sems.at[peer]))
        pending[-1].start()
    for copy in pending:
        copy.wait()


def select(wanted, planes):
    shape = (PLANE, 2 * Z, 32, 128)
    return pl.pallas_call(
        select_kernel,
        out_shape=jax.ShapeDtypeStruct(shape, jnp.bfloat16),
        in_specs=[SMEM_SPEC, VMEM_SPEC],
        out_specs=ANY_SPEC,
        scratch_shapes=[pltpu.VMEM(shape, jnp.bfloat16), pltpu.SemaphoreType.DMA((PLANE,))],
        compiler_params=pltpu.CompilerParams(vmem_limit_bytes=8 * MIB),
        cost_estimate=cost(1_000_000, 2_500_000),
        name="select",
    )(wanted, planes)


def near_kernel(
    near_list, own_row, signals, other, before, after, tiles, own_out, other_out, slot_out, extended, sems
):
    half, width = signals.shape
    reach = before.shape[1]
    leaf_count, near_count, leaf_size, _ = tiles.shape
    pending = load(
        [
            (before, extended.at[:, :reach]),
            (signals, extended.at[:half, reach : reach + width]),
            (other, extended.at[half:, reach : reach + width]),
            (after, extended.at[:, reach + width :]),
        ],
        sems,
    )
    for copy in pending:
        copy.wait()
    row = own_row[...]
    size = row.shape[1]
    at_col = lax.broadcasted_iota(jnp.int32, (size, size), 0)
    at_row = lax.broadcasted_iota(jnp.int32, (size, size), 1)
    column = jnp.sum(jnp.where(at_col == at_row, row, 0), axis=1, keepdims=True)
    earlier = jnp.where((column == row) & (at_col < at_row), 1, 0)
    seen = jnp.sum(earlier, axis=0, keepdims=True)
    slot_out[...] = row % PLANE * (2 * Z) + row // PLANE * 2 + seen
    loop, rhs = lax.axis_index("loop"), lax.axis_index("rhs")
    leaves = leaf_count * Z * PLANE
    for t in range(leaf_count):
        total = jnp.zeros((2 * half, leaf_size), jnp.float32)
        for j in range(near_count):
            source = near_list[t, rhs * near_count + j]
            at = (source - loop * leaf_count + leaf_count // 2 + leaves) % leaves
            block = extended[:, pl.ds(pl.multiple_of(at * leaf_size, leaf_size), leaf_size)]
            total = total + dot(block, tiles[t, j], NT)
        own_out[:, t * leaf_size : (t + 1) * leaf_size] = total[:half]
        other_out[:, t * leaf_size : (t + 1) * leaf_size] = total[half:].astype(jnp.bfloat16)


def near_field(near_list, own_row, signals, other, before, after, tiles):
    half, width = signals.shape
    return pl.pallas_call(
        near_kernel,
        out_shape=(
            jax.ShapeDtypeStruct((half, width), jnp.float32),
            jax.ShapeDtypeStruct((half, width), jnp.bfloat16),
            jax.ShapeDtypeStruct(own_row.shape, jnp.int32),
        ),
        in_specs=[SMEM_SPEC, VMEM_SPEC, ANY_SPEC, ANY_SPEC, ANY_SPEC, ANY_SPEC, VMEM_SPEC],
        out_specs=(VMEM_SPEC,) * 3,
        scratch_shapes=[
            pltpu.VMEM((2 * half, 2 * width), jnp.bfloat16),
            pltpu.SemaphoreType.DMA((4,)),
        ],
        compiler_params=pltpu.CompilerParams(vmem_limit_bytes=12 * MIB),
        cost_estimate=cost(600_000_000, 10_000_000),
        name="near_field",
    )(near_list, own_row, signals, other, before, after, tiles)


def fields_kernel(parent, parent_far, *refs):
    sources = refs[:10]
    coupling, transfer, out, parents = refs[10:]
    at = 0
    for ref in sources:
        parents[at : at + ref.shape[0]] = ref[...]
        at += ref.shape[0]
    me = lax.axis_index("loop")
    own_plane = me % PLANE
    per = 2 * Y * X
    columns = out.shape[2]
    results = []
    for p in range(parent_far.shape[0]):
        stacked = []
        for j in range(parent_far.shape[1]):
            source = parent_far[p, j]
            device = source // 2
            hop = jnp.bitwise_and(device // PLANE - me // PLANE + Z, Z - 1)
            dy = jnp.bitwise_and(device // (X * C) - own_plane // (X * C) + Y, Y - 1)
            cross = jnp.bitwise_xor(device, own_plane)
            dx = jnp.bitwise_and(cross // C, X - 1)
            member = (dy * X + dx) * 2 + jnp.bitwise_and(source, 1)
            base = jnp.int32(0)
            for place, h in enumerate((0, 1, 7, 2, 6, 3, 5, 4)):
                base = jnp.where(hop == h, place * per, base)
            where = jnp.bitwise_and(cross, C - 1) * (Z * per) + base + member
            stacked += unpack(parents[where])
        field = dot(coupling[p], jnp.concatenate(stacked, axis=0), NN)
        results.append(field[:, :columns].astype(jnp.bfloat16))
    for c in range(transfer.shape[0]):
        field = jnp.where(parent[c] == me * 2, results[0], results[1])
        out[c] = dot(transfer[c], field, NN)


def fields(parent, parent_far, pieces, parent_coupling, transfer):
    return pl.pallas_call(
        fields_kernel,
        out_shape=jax.ShapeDtypeStruct(transfer.shape, jnp.float32),
        in_specs=[SMEM_SPEC] * 2 + [VMEM_SPEC] * 12,
        out_specs=VMEM_SPEC,
        scratch_shapes=[pltpu.VMEM((2 * Z * Y * X * 2, 32, 128), jnp.bfloat16)],
        compiler_params=pltpu.CompilerParams(vmem_limit_bytes=16 * MIB),
        cost_estimate=cost(50_000_000, 4_000_000),
        name="fields",
    )(parent, parent_far, *pieces, parent_coupling, transfer)


def downward_kernel(
    slots_in,
    blocks_in,
    coupling_in,
    descended_in,
    basis_in,
    near_own_in,
    out_hbm,
    slots,
    blocks,
    coupling,
    descended,
    basis,
    near_own,
    stacked,
    out,
    sems,
    out_sems,
):
    leaf_count, rank, leaf_size = basis.shape
    part = blocks.shape[0] // 8
    pending = load(
        [(blocks_in.at[pl.ds(i * part, part)], blocks.at[pl.ds(i * part, part)]) for i in range(8)]
        + [(coupling_in.at[c], coupling.at[c]) for c in range(leaf_count)]
        + [(descended_in, descended), (basis_in, basis), (near_own_in, near_own), (slots_in, slots)],
        sems,
    )
    for copy in pending[:8] + pending[-1:]:
        copy.wait()
    sources = coupling.shape[2] // rank
    columns = out.shape[0]
    for c in range(leaf_count):
        for j in range(sources):
            pieces = jnp.concatenate(unpack(blocks[slots[0, c * sources + j]]), axis=0)
            stacked[c, j * rank : (j + 1) * rank] = pieces
    for copy in pending[8:-1]:
        copy.wait()
    far = [dot(coupling[c], stacked[c], NN)[:, :columns] for c in range(leaf_count)]
    combined = [(far[c] + descended[c]).astype(jnp.bfloat16) for c in range(leaf_count)]
    written = []
    for c in range(leaf_count):
        at = pl.ds(c * leaf_size, leaf_size)
        out[:, at] = near_own[:, at] + dot(combined[c], basis[c], TN)
        written.append(pltpu.make_async_copy(out.at[:, at], out_hbm.at[:, at], out_sems.at[c]))
        written[-1].start()
    for copy in written:
        copy.wait()


def downward(slots, blocks, coupling, descended, basis, near_own):
    arrays = (blocks, coupling, descended, basis, near_own)
    leaf_count = basis.shape[0]
    return pl.pallas_call(
        downward_kernel,
        out_shape=jax.ShapeDtypeStruct(near_own.shape, jnp.float32),
        in_specs=[ANY_SPEC] * 6,
        out_specs=ANY_SPEC,
        scratch_shapes=[pltpu.SMEM(slots.shape, jnp.int32)]
        + [pltpu.VMEM(a.shape, a.dtype) for a in arrays]
        + [
            pltpu.VMEM((leaf_count, coupling.shape[2], 128), jnp.bfloat16),
            pltpu.VMEM(near_own.shape, jnp.float32),
            pltpu.SemaphoreType.DMA((12 + leaf_count,)),
            pltpu.SemaphoreType.DMA((leaf_count,)),
        ],
        compiler_params=pltpu.CompilerParams(vmem_limit_bytes=62 * MIB),
        cost_estimate=cost(150_000_000, 6_000_000),
        name="downward",
    )(slots, *arrays)


def shards(
    signals,
    near_tiles,
    near_list,
    leaf_basis,
    transfer,
    parent,
    coupling,
    far_list,
    parent_coupling,
    parent_far,
):
    width = signals.shape[1]
    leaf_count = leaf_basis.shape[0]
    along = functools.partial(lax.ppermute, axis_name="loop")
    swap = functools.partial(lax.ppermute, axis_name="rhs", perm=[(0, 1), (1, 0)])
    x_swap = loop_moves(lambda z, y, x, c: (z, y, 1 - x, c))
    c_swap = loop_moves(lambda z, y, x, c: (z, y, x, 1 - c))
    columns_of = [[z * PLANE + p for z in range(Z)] for p in range(PLANE)]
    planes_of = [[z * PLANE + p for p in range(PLANE)] for z in range(Z)]

    other = swap(signals)
    peer_list = along(far_list, perm=c_swap)
    coefs, payload, own_row = upward(parent, far_list, peer_list, signals, leaf_basis, transfer)

    planes = lax.all_to_all(coefs, "loop", 0, 0, tiled=True, axis_index_groups=columns_of)
    pair = jnp.stack([payload, along(payload, perm=x_swap)])
    quads = jnp.stack(
        [pair]
        + [
            along(pair, perm=loop_moves(lambda z, y, x, c, dy=dy: (z, y - dy, x, c)))
            for dy in range(1, Y)
        ]
    )
    plane_lists = quads[:, :, 64:72].reshape(PLANE, 4, 128).transpose(1, 0, 2)
    parents = quads[:, :, :64].reshape(-1, 32, 128)
    down = functools.partial(along, perm=loop_moves(lambda z, y, x, c: (z - 1, y, x, c)))
    up = functools.partial(along, perm=loop_moves(lambda z, y, x, c: (z + 1, y, x, c)))
    one_down, one_up = down(parents), up(parents)

    other, late = lax.optimization_barrier((other, signals))
    reach = width // 2
    count = Z * PLANE
    before = along(
        jnp.concatenate([late[:, reach:], other[:, reach:]]), perm=[(i, (i + 1) % count) for i in range(count)]
    )
    after = along(
        jnp.concatenate([late[:, :reach], other[:, :reach]]), perm=[((i + 1) % count, i) for i in range(count)]
    )
    wanted = tables(plane_lists.astype(jnp.int32))
    send = select(wanted, planes)
    _, one_down, one_up, before, after = lax.optimization_barrier((send, one_down, one_up, before, after))
    blocks = lax.all_to_all(send, "loop", 0, 0, tiled=True, axis_index_groups=planes_of)

    two_down, two_up = down(one_down), up(one_up)
    near_own, near_other, slots = near_field(near_list, own_row, signals, other, before, after, near_tiles)
    near_in = swap(near_other)
    _, two_down, two_up = lax.optimization_barrier((near_other, two_down, two_up))
    three_down, three_up = down(two_down), up(two_up)
    half = parents.shape[0] // 2
    four_down = along(two_down[:half], perm=loop_moves(lambda z, y, x, c: (z - 2, y, x, c)))
    four_up = along(two_up[half:], perm=loop_moves(lambda z, y, x, c: (z + 2, y, x, c)))
    mine = [parents, one_down, one_up, two_down, two_up, three_down, three_up, four_down, four_up]
    theirs = [along(jnp.concatenate(mine), perm=c_swap)]
    descended = fields(parent, parent_far, mine + theirs, parent_coupling, transfer)

    partial = downward(slots, blocks.reshape(-1, 32, 128), coupling, descended, leaf_basis, near_own)
    return (partial + near_in.astype(jnp.float32)).astype(jnp.bfloat16)


def solution(mesh):
    in_specs = (
        P("rhs", "loop"),
        P("loop", "rhs", None, None),
        P("loop", None),
        P("loop", None, None),
        P("loop", None, None),
        P("loop"),
        P("loop", None, None),
        P("loop", None),
        P("loop", None, None),
        P("loop", None),
    )
    out_specs = P("rhs", "loop")
    return jax.shard_map(shards, mesh=mesh, in_specs=in_specs, out_specs=out_specs, check_vma=False)
```
